32 devices in a mesh: dp: 8 (over z, y), seq: 4 (over x, core).
Axes of the slice: x: 2, y: 2, z: 4, core: 2. Of those that a mesh axis runs over, the one named last changes fastest.
Arguments:
- inputs: bfloat16 [16, 1024, 1024], P('dp', 'seq'), may hold values from -6 to 6
- segments: int32 [16, 1024], P('dp', 'seq'), may hold values from 0 to 5, as said below
- cotangent: bfloat16 [16, 1024, 1024], P('dp', 'seq'), may hold values from -6 to 6
- ln1_gain: bfloat16 [1024], P(('dp', 'seq')), may hold values from 0.5 to 1.5
- ln1_shift: bfloat16 [1024], P(('dp', 'seq')), may hold values from -1.5 to 1.5
- qkv_weight: bfloat16 [1024, 3072], P(('dp', 'seq')), may hold values from -0.1875 to 0.1875
- qv_bias: bfloat16 [2, 1024], P(None, ('dp', 'seq')), may hold values from -2.5 to 2.5
- out_weight: bfloat16 [1024, 1024], P(('dp', 'seq')), may hold values from -0.75 to 0.75
- out_bias: bfloat16 [1024], P(('dp', 'seq')), may hold values from -2.5 to 2.5
- ln2_gain: bfloat16 [1024], P(('dp', 'seq')), may hold values from 0.5 to 1.5
- ln2_shift: bfloat16 [1024], P(('dp', 'seq')), may hold values from -1.5 to 1.5
- up_weight: bfloat16 [1024, 4096], P(('dp', 'seq')), may hold values from -0.1875 to 0.1875
- up_bias: bfloat16 [4096], P(('dp', 'seq')), may hold values from -2.5 to 2.5
- down_weight: bfloat16 [4096, 1024], P(('dp', 'seq')), may hold values from -0.09375 to 0.09375
- down_bias: bfloat16 [1024], P(('dp', 'seq')), may hold values from -2.5 to 2.5
Outputs:
- outputs: bfloat16 [16, 1024, 1024], P('dp', 'seq')
- input_grad: float32 [16, 1024, 1024], P('dp', 'seq')
- ln1_gain_grad: float32 [1024], P(('dp', 'seq'))
- ln1_shift_grad: float32 [1024], P(('dp', 'seq'))
- qkv_weight_grad: float32 [1024, 3072], P(('dp', 'seq'))
- qv_bias_grad: float32 [2, 1024], P(None, ('dp', 'seq'))
- out_weight_grad: float32 [1024, 1024], P(('dp', 'seq'))
- out_bias_grad: float32 [1024], P(('dp', 'seq'))
- ln2_gain_grad: float32 [1024], P(('dp', 'seq'))
- ln2_shift_grad: float32 [1024], P(('dp', 'seq'))
- up_weight_grad: float32 [1024, 4096], P(('dp', 'seq'))
- up_bias_grad: float32 [4096], P(('dp', 'seq'))
- down_weight_grad: float32 [4096, 1024], P(('dp', 'seq'))
- down_bias_grad: float32 [1024], P(('dp', 'seq'))
The draws below stay inside these ranges and needn't reach their ends.
Inputs may be any that keep to these rules, and one draw needn't show every extreme that they name: `segments`: along each sequence the numbers start at 0 and rise by one where a document ends; every document except a sequence's last holds 200 tokens or more.
All inputs are finite; a program needn't handle non-finite values.
Results may differ from the reference program's by a relative error of at most 0.012.
Values may be sent and summed in bfloat16 or wider, within the bound.
No kernel may reach another device: no remote copies, remote signals or barrier semaphores. Data moves between devices by JAX's collectives and lax.ppermute only.
A program may use at most 256 MiB of HBM per device.

```python
import jax
import jax.numpy as jnp
from jax import lax

D = 1024
HEAD_DIM = 64
FF = 4096
LEN = 1024
DOC_MIN = 200
TOK_DEV = 512
SEQS_DEV = 2
SEQS = 16


def draw_segments(key, part):
    key = jax.random.fold_in(key, 7)
    first_key, second_key, third_key = jax.random.split(key, 3)
    count = LEN // DOC_MIN + 1
    pieces = jax.random.randint(first_key, (SEQS, count), DOC_MIN, LEN + 1, dtype=jnp.int32)
    bounds = jnp.cumsum(pieces, axis=1)
    places = jnp.arange(LEN, dtype=jnp.int32)
    seg_ids = jnp.sum((bounds[:, None, :] <= places[None, :, None]).astype(jnp.int32), axis=2)
    group_count = SEQS // SEQS_DEV
    picked = jax.random.randint(second_key, (group_count,), 0, SEQS_DEV, dtype=jnp.int32)
    chosen = jnp.arange(group_count, dtype=jnp.int32) * SEQS_DEV + picked
    rows_all = jnp.arange(SEQS, dtype=jnp.int32)
    regular_row = (picked[0] + 1) % SEQS_DEV
    regular = (rows_all == regular_row) & (SEQS_DEV > 1)
    even_ids = places // DOC_MIN
    seg_ids = jnp.where(regular[:, None], even_ids[None, :], seg_ids)
    shard = TOK_DEV // SEQS_DEV
    cuts = jax.random.randint(third_key, (SEQS,), LEN - shard + 1, LEN, dtype=jnp.int32)
    spanning = (places[None, :] >= cuts[:, None]).astype(jnp.int32)
    whole = jnp.any(rows_all[:, None] == chosen[None, :], axis=1)
    return jnp.where(whole[:, None], spanning, seg_ids).astype(jnp.int32)


def levels(own_key, extent, shards, low, largest):
    level = 1.0
    for dim, shards_of in shards:
        heights = jax.random.uniform(jax.random.fold_in(jax.random.fold_in(own_key, 6), dim), (shards_of,), jnp.float32, low / len(shards), largest / len(shards))
        level = level * jnp.repeat(jnp.exp(heights), extent[dim] // shards_of).reshape((-1,) + (1,) * (len(extent) - 1 - dim))
    return level


def scatter_about(stream_key, shape, deviation, reach, shards=(), kind=jnp.bfloat16):
    drawn = deviation * jax.random.normal(stream_key, shape, jnp.float32)
    if shards:
        drawn = drawn * levels(stream_key, shape, shards, -0.22, 0.18)
    return jnp.clip(drawn, -reach, reach).astype(kind)


def setup_inputs(seed: int = 0) -> dict:
    arg_keys = jax.random.split(jax.random.key(seed), 16)
    return {
        "inputs": scatter_about(arg_keys[0], (SEQS, LEN, D), 1.0, 6.0, ((0, 8), (1, 4))),
        "segments": draw_segments(jax.random.fold_in(arg_keys[15], 71), 0),
        "cotangent": scatter_about(arg_keys[2], (SEQS, LEN, D), 1.0, 6.0, ((0, 8), (1, 4))),
        "ln1_gain": jnp.clip(1.0 + 0.1 * jax.random.normal(arg_keys[3], (D,), jnp.float32), 0.5, 1.5).astype(jnp.bfloat16),
        "ln1_shift": scatter_about(arg_keys[4], (D,), 0.3, 1.5, ((0, 32),)),
        "qkv_weight": scatter_about(arg_keys[5], (D, 3 * D), D ** -0.5, 0.1875, ((0, 32),)),
        "qv_bias": scatter_about(arg_keys[6], (2, D), 0.5, 2.5, ((1, 32),)),
        "out_weight": scatter_about(arg_keys[7], (D, D), (D // 16) ** -0.5, 0.75, ((0, 32),)),
        "out_bias": scatter_about(arg_keys[8], (D,), 0.5, 2.5, ((0, 32),)),
        "ln2_gain": jnp.clip(1.0 + 0.1 * jax.random.normal(arg_keys[9], (D,), jnp.float32), 0.5, 1.5).astype(jnp.bfloat16),
        "ln2_shift": scatter_about(arg_keys[10], (D,), 0.3, 1.5, ((0, 32),)),
        "up_weight": scatter_about(arg_keys[11], (D, FF), D ** -0.5, 0.1875, ((0, 32),)),
        "up_bias": scatter_about(arg_keys[12], (FF,), 0.5, 2.5, ((0, 32),)),
        "down_weight": scatter_about(arg_keys[13], (FF, D), FF ** -0.5, 0.09375, ((0, 32),)),
        "down_bias": scatter_about(arg_keys[14], (D,), 0.5, 2.5, ((0, 32),)),
    }


@jax.custom_vjp
def low(v):
    return lax.optimization_barrier(v.astype(jnp.bfloat16)).astype(jnp.float32)

@jax.custom_vjp
def low_back(v):
    return v

def low_keep(v):
    return (low(v), None)

def low_pass(kept, grad):
    return (grad,)

def back_keep(v):
    return (v, None)

def back_low(kept, grad):
    return (low(grad),)
low.defvjp(low_keep, low_pass)
low_back.defvjp(back_keep, back_low)

def norm_forward(values, gain, shift):
    average = lax.optimization_barrier(jnp.mean(values, axis=-1, keepdims=True))
    centred = values - average
    spread = lax.optimization_barrier(jnp.mean(centred * centred, axis=-1, keepdims=True))
    return centred * lax.rsqrt(spread + 1e-05) * gain + shift

def project(left, weight):
    return jnp.einsum('gtd,de->gte', left, weight, precision=lax.Precision.HIGHEST)

def forward(params, values, seg_ids):
    gain1, shift1, w_qkv, b_qv, w_out, b_out, gain2, shift2, w_up, b_up, w_down, b_down = params
    groups, length, width = values.shape
    heads = width // HEAD_DIM
    highest = lax.Precision.HIGHEST
    normed1 = low(norm_forward(values, gain1, shift1))
    bias_full = jnp.concatenate([b_qv[0], jnp.zeros((width,), jnp.float32), b_qv[1]])
    joined = low(low_back(project(normed1, w_qkv) + bias_full))
    queries = joined[..., :width].reshape(groups, length, heads, HEAD_DIM)
    keys = joined[..., width:2 * width].reshape(groups, length, heads, HEAD_DIM)
    vals = joined[..., 2 * width:].reshape(groups, length, heads, HEAD_DIM)
    scores = jnp.einsum('gqhd,gkhd->ghqk', queries, keys, precision=highest) * HEAD_DIM ** (-0.5)
    scores = low_back(scores)
    places = jnp.arange(length, dtype=jnp.int32)
    allowed = (seg_ids[:, :, None] == seg_ids[:, None, :]) & (places[None, None, :] <= places[None, :, None])
    scores = jnp.where(allowed[:, None], scores, -1000000000.0)
    weights = low(jax.nn.softmax(scores, axis=-1))
    attended = jnp.einsum('ghqk,gkhd->gqhd', weights, vals, precision=highest).reshape(groups, length, width)
    attended = low(low_back(attended))
    resid = values + low_back(project(attended, w_out) + b_out)
    normed2 = low(norm_forward(resid, gain2, shift2))
    pre = low_back(project(normed2, w_up) + b_up)
    active = low(jax.nn.gelu(pre, approximate=True))
    mixed = low_back(project(active, w_down) + b_down)
    return resid + mixed

def reference(inputs, segments, cotangent, ln1_gain, ln1_shift, qkv_weight, qv_bias, out_weight, out_bias, ln2_gain, ln2_shift, up_weight, up_bias, down_weight, down_bias):
    params = tuple((p.astype(jnp.float32) for p in (ln1_gain, ln1_shift, qkv_weight, qv_bias, out_weight, out_bias, ln2_gain, ln2_shift, up_weight, up_bias, down_weight, down_bias)))
    limit = max(1, 4096 // LEN)
    group = 1
    for option in range(1, SEQS + 1):
        if SEQS % option == 0 and option <= limit:
            group = option
    blocks = SEQS // group
    values_all = inputs.astype(jnp.float32).reshape(blocks, group, LEN, D)
    seg_all = segments.reshape(blocks, group, LEN)
    grads_all = cotangent.astype(jnp.float32).reshape(blocks, group, LEN, D)

    def step(totals, item):
        values, seg_ids, grad_out = item
        result, pullback = jax.vjp(lambda p, v: forward(p, v, seg_ids), params, values)
        grad_params, grad_values = pullback(grad_out)
        totals = jax.tree.map(lambda a, b: a + b, totals, grad_params)
        return (totals, (result.astype(jnp.bfloat16), grad_values))
    start = jax.tree.map(jnp.zeros_like, params)
    totals, (results, grad_inputs) = lax.scan(step, start, (values_all, seg_all, grads_all))
    return (results.reshape(SEQS, LEN, D), grad_inputs.reshape(SEQS, LEN, D), totals[0], totals[1], totals[2], totals[3], totals[4], totals[5], totals[6], totals[7], totals[8], totals[9], totals[10], totals[11])
```

```python
import functools

import jax
import jax.numpy as jnp
from jax import lax
from jax.experimental import pallas as pl
from jax.experimental.pallas import tpu as pltpu
from jax.sharding import Mesh
from jax.sharding import PartitionSpec as P

HEAD_DIM = 64
PAIR = 2 * HEAD_DIM
LANES = 128
BLOCK = 256
SWAP = [(0, 1), (1, 0)]
CHIPS = ("z", "y", "x")
BF16 = jnp.bfloat16
F32 = jnp.float32


def norm_forward(values, gain, shift):
    average = jnp.mean(values, axis=-1, keepdims=True)
    centred = values - average
    spread = jnp.mean(centred * centred, axis=-1, keepdims=True)
    return centred * lax.rsqrt(spread + 1e-05) * gain + shift


def gelu_tanh(values):
    return jax.nn.gelu(values, approximate=True)


def dot_plain(left, right):
    return jnp.dot(left, right, preferred_element_type=F32)


def dot_outer(left, right):
    return lax.dot_general(left, right, (((0,), (0,)), ((), ())), preferred_element_type=F32)


def dot_back(left, weight):
    return lax.dot_general(left, weight, (((1,), (1,)), ((), ())), preferred_element_type=F32)


def fill_bias(seg_keys, seg_queries, bias):
    total = bias.shape[0]
    for start in range(0, total, BLOCK):
        stop = start + BLOCK
        places_k = lax.broadcasted_iota(jnp.int32, (stop, BLOCK), 0)
        places_q = lax.broadcasted_iota(jnp.int32, (stop, BLOCK), 1) + start
        kept = (seg_keys[:stop, :] == seg_queries[:, start:stop]) & (places_k <= places_q)
        bias[:stop, start:stop] = jnp.where(kept, 0.0, -1000000000.0)


def head_masks():
    lanes = lax.broadcasted_iota(jnp.int32, (1, PAIR), 1)
    return [(lanes // HEAD_DIM == head).astype(F32).astype(BF16) for head in range(2)]


def turned(values):
    return values.astype(F32).T.astype(BF16)


def forward_kernel(seg_keys, seg_queries, qkv, out, logsum, bias):
    step = pl.program_id(0)
    total = out.shape[0]
    width = out.shape[1]

    @pl.when(step == 0)
    def _():
        fill_bias(seg_keys, seg_queries, bias)

    column = pl.multiple_of(step * PAIR, PAIR)
    keys = qkv[:, pl.ds(width + column, PAIR)]
    values_t = turned(qkv[:, pl.ds(2 * width + column, PAIR)])
    masks = head_masks()
    for start in range(0, total, BLOCK):
        stop = start + BLOCK
        queries = qkv[start:stop, pl.ds(column, PAIR)] * jnp.asarray(HEAD_DIM ** (-0.5), BF16)
        parts = []
        for head in range(2):
            scores = dot_back(keys[:stop], queries * masks[head]) + bias[:stop, start:stop]
            highest = jnp.max(scores, axis=0, keepdims=True)
            expon = jnp.exp(scores - highest)
            totals = jnp.sum(expon, axis=0, keepdims=True)
            first = head * HEAD_DIM
            part = dot_plain(values_t[first : first + HEAD_DIM, :stop], expon.astype(BF16))
            parts.append(part / totals)
            logsum[0, head : head + 1, start:stop] = highest + jnp.log(totals)
        out[start:stop, pl.ds(column, PAIR)] = jnp.concatenate(parts, axis=0).T.astype(BF16)


def backward_kernel(seg_keys, seg_queries, qkv, grad, logsum, grad_qkv, bias, sum_k, sum_v):
    step = pl.program_id(0)
    total, width = grad.shape

    @pl.when(step == 0)
    def _():
        fill_bias(seg_keys, seg_queries, bias)

    column = pl.multiple_of(step * PAIR, PAIR)
    keys = qkv[:, pl.ds(width + column, PAIR)]
    values = qkv[:, pl.ds(2 * width + column, PAIR)]
    keys_t = turned(keys)
    masks = head_masks()
    sum_k[...] = jnp.zeros_like(sum_k)
    sum_v[...] = jnp.zeros_like(sum_v)
    for start in range(0, total, BLOCK):
        stop = start + BLOCK
        queries = qkv[start:stop, pl.ds(column, PAIR)] * jnp.asarray(HEAD_DIM ** (-0.5), BF16)
        grads = grad[start:stop, pl.ds(column, PAIR)]
        parts = []
        for head in range(2):
            query = queries * masks[head]
            grad_head = grads * masks[head]
            scores = dot_back(keys[:stop], query) + bias[:stop, start:stop]
            weights = jnp.exp(scores - logsum[0, head : head + 1, start:stop])
            grad_weights = dot_back(values[:stop], grad_head)
            inner = jnp.sum(weights * grad_weights, axis=0, keepdims=True)
            grad_scores = (weights * (grad_weights - inner)).astype(BF16)
            sum_v[:stop, :] += dot_plain(weights.astype(BF16), grad_head)
            sum_k[:stop, :] += dot_plain(grad_scores, query)
            first = head * HEAD_DIM
            parts.append(dot_plain(keys_t[first : first + HEAD_DIM, :stop], grad_scores))
        grad_queries = jnp.concatenate(parts, axis=0).T * HEAD_DIM ** (-0.5)
        grad_qkv[start:stop, pl.ds(column, PAIR)] = grad_queries.astype(BF16)
    grad_qkv[:, pl.ds(width + column, PAIR)] = sum_k[...].astype(BF16)
    grad_qkv[:, pl.ds(2 * width + column, PAIR)] = sum_v[...].astype(BF16)


def whole_block(shape):
    return pl.BlockSpec(shape, lambda step: (0,) * len(shape))


def attend(seg_keys, seg_queries, qkv):
    total, width3 = qkv.shape
    width = width3 // 3
    pairs = width // PAIR
    return pl.pallas_call(
        forward_kernel,
        grid=(pairs,),
        in_specs=[whole_block((total, 1)), whole_block((1, total)), whole_block((total, width3))],
        out_specs=[
            whole_block((total, width)),
            pl.BlockSpec((1, 2, total), lambda step: (step, 0, 0)),
        ],
        out_shape=[
            jax.ShapeDtypeStruct((total, width), BF16),
            jax.ShapeDtypeStruct((pairs, 2, total), F32),
        ],
        scratch_shapes=[pltpu.VMEM((total, total), F32)],
        compiler_params=pltpu.CompilerParams(vmem_limit_bytes=48 * 1024 * 1024),
        cost_estimate=pl.CostEstimate(
            flops=8 * total * total * width, bytes_accessed=10 * total * width, transcendentals=0
        ),
        name="attention_forward",
    )(seg_keys, seg_queries, qkv)


def attend_back(seg_keys, seg_queries, qkv, grad, logsum):
    total, width = grad.shape
    pairs = width // PAIR
    return pl.pallas_call(
        backward_kernel,
        grid=(pairs,),
        in_specs=[
            whole_block((total, 1)),
            whole_block((1, total)),
            whole_block((total, 3 * width)),
            whole_block((total, width)),
            pl.BlockSpec((1, 2, total), lambda step: (step, 0, 0)),
        ],
        out_specs=whole_block((total, 3 * width)),
        out_shape=jax.ShapeDtypeStruct((total, 3 * width), BF16),
        scratch_shapes=[
            pltpu.VMEM((total, total), F32),
            pltpu.VMEM((total, PAIR), F32),
            pltpu.VMEM((total, PAIR), F32),
        ],
        compiler_params=pltpu.CompilerParams(vmem_limit_bytes=48 * 1024 * 1024),
        cost_estimate=pl.CostEstimate(
            flops=20 * total * total * width, bytes_accessed=20 * total * width, transcendentals=0
        ),
        name="attention_backward",
    )(seg_keys, seg_queries, qkv, grad, logsum)


def swap_core(array):
    return lax.ppermute(array, "c", SWAP)


def take(array, place, axis=0):
    return lax.dynamic_index_in_dim(array, place, axis, keepdims=False)


def in_order(place, own, other, axis):
    first = jnp.stack([own, other], axis=axis)
    second = jnp.stack([other, own], axis=axis)
    return jnp.where(place == 0, first, second)


def over_x(array):
    count = lax.axis_size("x")
    if count != 2:
        return lax.all_to_all(array, "x", 0, 0)
    here = lax.axis_index("x")
    other = lax.ppermute(take(array, 1 - here), "x", SWAP)
    return in_order(here, take(array, here), other, 0)


def plane_split():
    return lax.axis_size("x") == 2 and lax.axis_size("y") == 2


def gather_chips(chunk):
    if not plane_split():
        full = lax.all_gather(chunk, CHIPS)
        sizes = tuple(lax.axis_size(name) for name in CHIPS)
        return full.reshape(sizes + chunk.shape)
    line = lax.all_gather(chunk, "z")
    y, x = lax.axis_index("y"), lax.axis_index("x")
    half = chunk.shape[0] // 2
    from_x = lax.ppermute(line, "x", SWAP)
    from_y = lax.ppermute(line, "y", SWAP)
    corner_low = lax.ppermute(from_x[:, :half], "y", SWAP)
    corner_high = lax.ppermute(from_y[:, half:], "x", SWAP)
    full = jnp.zeros((line.shape[0], 2, 2) + chunk.shape, chunk.dtype)

    def put(full, part, py, px, row):
        return lax.dynamic_update_slice(full, part[:, None, None], (0, py, px, row, 0))

    full = put(full, line, y, x, 0)
    full = put(full, from_x, y, 1 - x, 0)
    full = put(full, from_y, 1 - y, x, 0)
    full = put(full, corner_low, 1 - y, 1 - x, 0)
    return put(full, corner_high, 1 - y, 1 - x, half)


def add_low(*parts):
    return functools.reduce(jnp.add, [part.astype(F32) for part in parts]).astype(BF16)


def scatter_chips(chunks):
    if not plane_split():
        return lax.psum_scatter(chunks, CHIPS, scatter_dimension=0)
    _, rows, columns = chunks.shape
    y, x = lax.axis_index("y"), lax.axis_index("x")
    split = chunks.reshape(-1, 2, 2, rows, columns)
    half = rows // 2

    def part(py, px, first, count):
        size = (split.shape[0], 1, 1, count, columns)
        return lax.dynamic_slice(split, (0, py, px, first, 0), size)[:, 0, 0]

    corner_x = lax.ppermute(part(1 - y, 1 - x, 0, half), "x", SWAP)
    corner_y = lax.ppermute(part(1 - y, 1 - x, half, half), "y", SWAP)
    to_y = jnp.concatenate(
        [add_low(part(1 - y, x, 0, half), corner_x), part(1 - y, x, half, half)], axis=1
    )
    to_x = jnp.concatenate(
        [part(y, 1 - x, 0, half), add_low(part(y, 1 - x, half, half), corner_y)], axis=1
    )
    from_x = lax.ppermute(to_x, "x", SWAP)
    from_y = lax.ppermute(to_y, "y", SWAP)
    total = add_low(part(y, x, 0, rows), from_x, from_y)
    return lax.psum_scatter(total, "z", scatter_dimension=0)


def per_device(
    inputs,
    segments,
    cotangent,
    ln1_gain,
    ln1_shift,
    qkv_weight,
    qv_bias,
    out_weight,
    out_bias,
    ln2_gain,
    ln2_shift,
    up_weight,
    up_bias,
    down_weight,
    down_bias,
):
    _, rows, width = inputs.shape
    own_rows = out_weight.shape[0]
    own_units = down_weight.shape[0]
    chips = width // (2 * own_rows)
    core = lax.axis_index("c")
    half = width // 2
    mine = 2 * chips * own_units // 2

    small = jnp.concatenate(
        [ln1_gain, ln1_shift, qv_bias[0], qv_bias[1], out_bias, ln2_gain, ln2_shift, down_bias, up_bias]
    )
    small_count = small.shape[0]
    small = jnp.pad(small, (0, own_rows * LANES - small_count)).reshape(own_rows, LANES)

    def head_columns(place):
        return [
            lax.dynamic_slice_in_dim(qkv_weight, part * width + place * half, half, 1)
            for part in range(3)
        ]

    send = jnp.concatenate(head_columns(1 - core) + [small], axis=1)
    keep = jnp.concatenate(head_columns(core) + [small], axis=1)
    chunk_qkv = in_order(core, keep, swap_core(send), 0).reshape(2 * own_rows, -1)
    up_split = up_weight.reshape(own_rows, chips, 2, own_units)
    up_keep = take(up_split, core, 2).reshape(own_rows, mine)
    up_send = take(up_split, 1 - core, 2).reshape(own_rows, mine)
    chunk_up = in_order(core, up_keep, swap_core(up_send), 0).reshape(2 * own_rows, -1)

    own_x = over_x(inputs)
    own_g = over_x(cotangent)
    own_seg = over_x(segments)

    def both_cores(array):
        joined = in_order(core, array, swap_core(array), 1)
        return joined.reshape((-1,) + array.shape[2:])

    def split_cores(array):
        parts = array.reshape(-1, 2, rows, array.shape[-1])
        return take(parts, core, 1), take(parts, 1 - core, 1)

    seg_all = both_cores(own_seg[..., None])
    seg_keys = seg_all
    seg_queries = seg_all.reshape(1, -1)
    full_x = both_cores(own_x).astype(F32)
    full_g = both_cores(own_g)

    all_qkv = gather_chips(chunk_qkv)
    w_qkv = all_qkv[..., : 3 * half].reshape(width, 3 * half)
    smalls = all_qkv[..., 3 * half :].reshape(2 * chips, -1)[:, :small_count]
    vectors = [
        smalls[:, place * own_rows : (place + 1) * own_rows].reshape(width).astype(F32)
        for place in range(8)
    ]
    gain1, shift1, b_q, b_v, b_out, gain2, shift2, b_down = vectors
    b_up = take(smalls[:, 8 * own_rows :].reshape(chips, 2, own_units), core, 1)
    b_up = b_up.reshape(mine).astype(F32)

    normed1 = norm_forward(full_x, gain1, shift1).astype(BF16)
    b_qkv = jnp.concatenate(
        [
            lax.dynamic_slice_in_dim(b_q, core * half, half),
            jnp.zeros((half,), F32),
            lax.dynamic_slice_in_dim(b_v, core * half, half),
        ]
    )
    qkv = (dot_plain(normed1, w_qkv) + b_qkv).astype(BF16)
    attended, logsum = attend(seg_keys, seg_queries, qkv)

    all_out = gather_chips(out_weight).reshape(chips, own_rows, width)
    out_keep = lax.dynamic_slice_in_dim(all_out, core * (chips // 2), chips // 2)
    out_send = lax.dynamic_slice_in_dim(all_out, (1 - core) * (chips // 2), chips // 2)
    w_out = in_order(core, out_keep, swap_core(out_send), 1).reshape(half, width)
    w_up = gather_chips(chunk_up).reshape(width, mine)
    w_down = gather_chips(down_weight).reshape(mine, width)

    def add_cores(partial):
        keep_part, send_part = split_cores(partial)
        return keep_part + swap_core(send_part.astype(BF16)).astype(F32)

    resid = own_x.astype(F32) + add_cores(dot_plain(attended, w_out)) + b_out
    normed2_own = norm_forward(resid, gain2, shift2).astype(BF16)
    normed2 = both_cores(normed2_own)
    pre = dot_plain(normed2, w_up) + b_up
    active = gelu_tanh(pre).astype(BF16)
    mixed = add_cores(dot_plain(active, w_down)) + b_down
    outputs = over_x((resid + mixed).astype(BF16))

    grad_down = dot_outer(active, full_g).astype(BF16)
    down_grad = scatter_chips(grad_down.reshape(chips, own_units, width)).astype(F32)
    grad_active = dot_back(full_g, w_down)
    _, gelu_pull = jax.vjp(gelu_tanh, pre)
    grad_pre = gelu_pull(grad_active)[0].astype(BF16)
    grad_up = dot_outer(normed2, grad_pre).astype(BF16)
    up_sum = scatter_chips(grad_up.reshape(chips, 2 * own_rows, mine)).reshape(2, own_rows, mine)
    up_other = swap_core(take(up_sum, 1 - core))
    up_grad = in_order(
        core,
        take(up_sum, core).reshape(own_rows, chips, own_units),
        up_other.reshape(own_rows, chips, own_units),
        2,
    )
    up_grad = up_grad.reshape(own_rows, 2 * mine).astype(F32)
    grad_normed2 = add_cores(dot_back(grad_pre, w_up))
    own_g32 = own_g.astype(F32)
    _, norm2_pull = jax.vjp(norm_forward, resid, gain2, shift2)
    grad_part, grad_gain2, grad_shift2 = norm2_pull(grad_normed2)
    grad_resid = own_g32 + grad_part

    grad_branch_own = grad_resid.astype(BF16)
    grad_branch = both_cores(grad_branch_own)
    grad_attended = dot_back(grad_branch, w_out).astype(BF16)
    grad_out = dot_outer(attended, grad_branch).astype(BF16)
    grad_out = grad_out.reshape(chips // 2, 2, own_rows, width)
    out_other = swap_core(take(grad_out, 1 - core, 1))
    out_terms = in_order(core, take(grad_out, core, 1), out_other, 0)
    out_grad = scatter_chips(out_terms.reshape(chips, own_rows, width)).astype(F32)

    grad_qkv = attend_back(seg_keys, seg_queries, qkv, grad_attended, logsum)
    grad_normed1 = add_cores(dot_back(grad_qkv, w_qkv))
    own_x32 = own_x.astype(F32)
    _, norm1_pull = jax.vjp(norm_forward, own_x32, gain1, shift1)
    grad_part1, grad_gain1, grad_shift1 = norm1_pull(grad_normed1)
    grad_x = grad_resid + grad_part1

    def place_heads(sums):
        zeros = jnp.zeros((width,), F32)
        return lax.dynamic_update_slice_in_dim(zeros, sums, core * half, 0)

    head_sums = jnp.sum(grad_qkv.astype(F32), axis=0)
    small_sums = [
        grad_gain1,
        grad_shift1,
        place_heads(head_sums[:half]),
        place_heads(head_sums[2 * half :]),
        jnp.sum(grad_branch_own.astype(F32), axis=(0, 1)),
        grad_gain2,
        grad_shift2,
        jnp.sum(own_g32, axis=(0, 1)),
    ]
    up_sums = jnp.sum(grad_pre.astype(F32), axis=0)
    small_terms = jnp.concatenate(
        [vector.reshape(chips, 2 * own_rows) for vector in small_sums]
        + [up_sums.reshape(chips, own_units)],
        axis=1,
    )
    small_width = small_terms.shape[1]
    small_terms = jnp.pad(small_terms, ((0, 0), (0, 2 * own_rows * LANES - small_width)))
    small_terms = small_terms.reshape(chips, 2 * own_rows, LANES).astype(BF16)
    grad_weight = dot_outer(normed1, grad_qkv).astype(BF16).reshape(chips, 2 * own_rows, 3 * half)
    qkv_sum = scatter_chips(jnp.concatenate([grad_weight, small_terms], axis=2))
    sums = qkv_sum[:, 3 * half :].reshape(-1)
    weight_sum = qkv_sum[:, : 3 * half].reshape(2, own_rows, 3 * half)
    qkv_other = swap_core(take(weight_sum, 1 - core))
    qkv_grad = in_order(
        core,
        take(weight_sum, core).reshape(own_rows, 3, half),
        qkv_other.reshape(own_rows, 3, half),
        2,
    )
    qkv_grad = qkv_grad.reshape(own_rows, 6 * half).astype(F32)
    shared = sums[: 16 * own_rows].reshape(8, 2, own_rows).astype(F32)
    shared = take(shared, core, 1) + swap_core(take(shared, 1 - core, 1))
    up_bias_grad = sums[16 * own_rows : 16 * own_rows + own_units].astype(F32)

    count = lax.axis_size("x")
    if count == 2:
        here = lax.axis_index("x")
        other = lax.ppermute(take(grad_x, 1 - here).astype(BF16), "x", SWAP).astype(F32)
        input_grad = in_order(here, take(grad_x, here), other, 0)
    else:
        input_grad = over_x(grad_x)
    return (
        outputs,
        input_grad,
        shared[0],
        shared[1],
        qkv_grad,
        shared[2:4],
        out_grad,
        shared[4],
        shared[5],
        shared[6],
        up_grad,
        up_bias_grad,
        down_grad,
        shared[7],
    )


def solution(mesh):
    groups, members = mesh.devices.shape
    split = Mesh(mesh.devices.reshape(groups // 2, 2, members // 2, 2), ("z", "y", "x", "c"))
    every = ("z", "y", "x", "c")
    tokens = P(("z", "y"), ("x", "c"), None)
    vector = P(every)
    matrix = P(every, None)
    return jax.shard_map(
        per_device,
        mesh=split,
        in_specs=(
            tokens,
            P(("z", "y"), ("x", "c")),
            tokens,
            vector,
            vector,
            matrix,
            P(None, every),
            matrix,
            vector,
            vector,
            vector,
            matrix,
            vector,
            matrix,
            vector,
        ),
        out_specs=(
            tokens,
            tokens,
            vector,
            vector,
            matrix,
            P(None, every),
            matrix,
            vector,
            vector,
            vector,
            matrix,
            vector,
            matrix,
            vector,
        ),
        check_vma=False,
    )
```

```python
import functools

import jax
import jax.numpy as jnp
from jax import lax
from jax.experimental import pallas as pl
from jax.experimental.pallas import tpu as pltpu
from jax.sharding import Mesh
from jax.sharding import PartitionSpec as P

HEAD_DIM = 64
PAIR = 2 * HEAD_DIM
LANES = 128
BLOCK = 256
SWAP = [(0, 1), (1, 0)]
CHIPS = ("z", "y", "x")
BF16 = jnp.bfloat16
F32 = jnp.float32


def norm_forward(values, gain, shift):
    average = jnp.mean(values, axis=-1, keepdims=True)
    centred = values - average
    spread = jnp.mean(centred * centred, axis=-1, keepdims=True)
    return centred * lax.rsqrt(spread + 1e-05) * gain + shift


def gelu_tanh(values):
    return jax.nn.gelu(values, approximate=True)


def dot_plain(left, right):
    return jnp.dot(left, right, preferred_element_type=F32)


def dot_outer(left, right):
    return lax.dot_general(left, right, (((0,), (0,)), ((), ())), preferred_element_type=F32)


def dot_back(left, weight):
    return lax.dot_general(left, weight, (((1,), (1,)), ((), ())), preferred_element_type=F32)


def fill_bias(seg_keys, seg_queries, bias):
    total = bias.shape[0]
    for start in range(0, total, BLOCK):
        stop = start + BLOCK
        places_k = lax.broadcasted_iota(jnp.int32, (stop, BLOCK), 0)
        places_q = lax.broadcasted_iota(jnp.int32, (stop, BLOCK), 1) + start
        kept = (seg_keys[:stop, :] == seg_queries[:, start:stop]) & (places_k <= places_q)
        bias[:stop, start:stop] = jnp.where(kept, 0.0, -1000000000.0)


def piece_rows(places, first, piece):
    return pl.ds(pl.multiple_of(places[first // piece], piece), piece)


def load_rows(places, source, first, count, columns):
    piece = source.shape[0] // places.shape[0]
    return jnp.concatenate(
        [
            source[piece_rows(places, start, piece), columns]
            for start in range(first, first + count, piece)
        ],
        axis=0,
    )


def store_rows(places, target, first, count, columns, rows):
    piece = target.shape[0] // places.shape[0]
    for start in range(0, count, piece):
        target[piece_rows(places, first + start, piece), columns] = rows[start : start + piece]


def head_masks():
    lanes = lax.broadcasted_iota(jnp.int32, (1, PAIR), 1)
    return [(lanes // HEAD_DIM == head).astype(F32).astype(BF16) for head in range(2)]


def turned(values):
    return values.astype(F32).T.astype(BF16)


def forward_kernel(places, seg_keys, seg_queries, qkv, out, logsum, bias):
    step = pl.program_id(0)
    total = out.shape[0]
    width = out.shape[1]

    @pl.when(step == 0)
    def _():
        fill_bias(seg_keys, seg_queries, bias)

    column = pl.multiple_of(step * PAIR, PAIR)
    here = pl.ds(column, PAIR)
    keys = load_rows(places, qkv, 0, total, pl.ds(width + column, PAIR))
    values_t = turned(load_rows(places, qkv, 0, total, pl.ds(2 * width + column, PAIR)))
    masks = head_masks()
    for start in range(0, total, BLOCK):
        stop = start + BLOCK
        queries = load_rows(places, qkv, start, BLOCK, here)
        queries = queries * jnp.asarray(HEAD_DIM ** (-0.5), BF16)
        parts = []
        for head in range(2):
            scores = dot_back(keys[:stop], queries * masks[head]) + bias[:stop, start:stop]
            highest = jnp.max(scores, axis=0, keepdims=True)
            expon = jnp.exp(scores - highest)
            totals = jnp.sum(expon, axis=0, keepdims=True)
            first = head * HEAD_DIM
            part = dot_plain(values_t[first : first + HEAD_DIM, :stop], expon.astype(BF16))
            parts.append(part / totals)
            logsum[0, head : head + 1, start:stop] = highest + jnp.log(totals)
        rows = jnp.concatenate(parts, axis=0).T.astype(BF16)
        store_rows(places, out, start, BLOCK, here, rows)


def backward_kernel(
    first_pair, places, seg_keys, seg_queries, qkv, grad, logsum, grad_qkv, bias, sum_k, sum_v
):
    step = pl.program_id(0)
    total, width = grad.shape

    @pl.when(step == 0)
    def _():
        fill_bias(seg_keys, seg_queries, bias)

    column = pl.multiple_of((first_pair + step) * PAIR, PAIR)
    here = pl.ds(column, PAIR)
    here_k = pl.ds(width + column, PAIR)
    here_v = pl.ds(2 * width + column, PAIR)
    part_width = grad_qkv.shape[1] // 3
    part_column = pl.multiple_of(step * PAIR, PAIR)
    put_q = pl.ds(part_column, PAIR)
    put_k = pl.ds(part_width + part_column, PAIR)
    put_v = pl.ds(2 * part_width + part_column, PAIR)
    keys = load_rows(places, qkv, 0, total, here_k)
    values = load_rows(places, qkv, 0, total, here_v)
    keys_t = turned(keys)
    masks = head_masks()
    sum_k[...] = jnp.zeros_like(sum_k)
    sum_v[...] = jnp.zeros_like(sum_v)
    for start in range(0, total, BLOCK):
        stop = start + BLOCK
        queries = load_rows(places, qkv, start, BLOCK, here)
        queries = queries * jnp.asarray(HEAD_DIM ** (-0.5), BF16)
        grads = load_rows(places, grad, start, BLOCK, here)
        parts = []
        for head in range(2):
            query = queries * masks[head]
            grad_head = grads * masks[head]
            scores = dot_back(keys[:stop], query) + bias[:stop, start:stop]
            weights = jnp.exp(scores - logsum[0, head : head + 1, start:stop])
            grad_weights = dot_back(values[:stop], grad_head)
            inner = jnp.sum(weights * grad_weights, axis=0, keepdims=True)
            grad_scores = (weights * (grad_weights - inner)).astype(BF16)
            sum_v[:stop, :] += dot_plain(weights.astype(BF16), grad_head)
            sum_k[:stop, :] += dot_plain(grad_scores, query)
            first = head * HEAD_DIM
            parts.append(dot_plain(keys_t[first : first + HEAD_DIM, :stop], grad_scores))
        grad_queries = jnp.concatenate(parts, axis=0).T * HEAD_DIM ** (-0.5)
        store_rows(places, grad_qkv, start, BLOCK, put_q, grad_queries.astype(BF16))
    store_rows(places, grad_qkv, 0, total, put_k, sum_k[...].astype(BF16))
    store_rows(places, grad_qkv, 0, total, put_v, sum_v[...].astype(BF16))


def whole_block(shape):
    return pl.BlockSpec(shape, lambda step: (0,) * len(shape))


def attend(places, seg_keys, seg_queries, qkv):
    total, width3 = qkv.shape
    width = width3 // 3
    pairs = width // PAIR
    return pl.pallas_call(
        forward_kernel,
        grid=(pairs,),
        in_specs=[
            pl.BlockSpec(memory_space=pltpu.SMEM),
            whole_block((total, 1)),
            whole_block((1, total)),
            whole_block((total, width3)),
        ],
        out_specs=[
            whole_block((total, width)),
            pl.BlockSpec((1, 2, total), lambda step: (step, 0, 0)),
        ],
        out_shape=[
            jax.ShapeDtypeStruct((total, width), BF16),
            jax.ShapeDtypeStruct((pairs, 2, total), F32),
        ],
        scratch_shapes=[pltpu.VMEM((total, total), F32)],
        compiler_params=pltpu.CompilerParams(vmem_limit_bytes=48 * 1024 * 1024),
        cost_estimate=pl.CostEstimate(
            flops=40 * total * total * width, bytes_accessed=total * width, transcendentals=0
        ),
        name="attention_forward",
    )(places, seg_keys, seg_queries, qkv)


def attend_back(places, seg_keys, seg_queries, qkv, grad, logsum, first, pairs):
    total, width = grad.shape
    return pl.pallas_call(
        functools.partial(backward_kernel, first),
        grid=(pairs,),
        in_specs=[
            pl.BlockSpec(memory_space=pltpu.SMEM),
            whole_block((total, 1)),
            whole_block((1, total)),
            whole_block((total, 3 * width)),
            whole_block((total, width)),
            pl.BlockSpec((1, 2, total), lambda step: (first + step, 0, 0)),
        ],
        out_specs=whole_block((total, 3 * pairs * PAIR)),
        out_shape=jax.ShapeDtypeStruct((total, 3 * pairs * PAIR), BF16),
        scratch_shapes=[
            pltpu.VMEM((total, total), F32),
            pltpu.VMEM((total, PAIR), F32),
            pltpu.VMEM((total, PAIR), F32),
        ],
        compiler_params=pltpu.CompilerParams(vmem_limit_bytes=48 * 1024 * 1024),
        cost_estimate=pl.CostEstimate(
            flops=total * total, bytes_accessed=total * width, transcendentals=0
        ),
        name="attention_backward",
    )(places, seg_keys, seg_queries, qkv, grad, logsum)


def pack_kernel(core, qkv, up, segments, *refs):
    vectors, (send_qkv, keep_qkv, send_up, keep_up) = refs[:-4], refs[-4:]
    rows, width3 = qkv.shape
    half = width3 // 6
    blocks = up.shape[1] // (2 * LANES)
    for place, to_qkv, to_up in ((1 - core[0], send_qkv, send_up), (core[0], keep_qkv, keep_up)):
        for part in range(3):
            start = pl.multiple_of(2 * part * half + place * half, half)
            to_qkv[:, part * half : (part + 1) * half] = qkv[:, pl.ds(start, half)]
        to_qkv[:, 3 * half :] = jnp.zeros((rows, LANES), BF16)
        row = 0
        for vector in vectors:
            count, size = vector.shape
            to_qkv[row : row + count, 3 * half : 3 * half + size] = vector[...]
            row += count
        for sequence in range(segments.shape[0]):
            for start in range(0, segments.shape[1], LANES):
                numbers = segments[sequence : sequence + 1, start : start + LANES]
                to_qkv[row : row + 1, 3 * half :] = numbers.astype(F32).astype(BF16)
                row += 1
        for block in range(blocks):
            start = pl.multiple_of((2 * block + place) * LANES, LANES)
            to_up[:, block * LANES : (block + 1) * LANES] = up[:, pl.ds(start, LANES)]


def pack(core, qkv, up, segments, vectors):
    rows = qkv.shape[0]
    shape_qkv = jax.ShapeDtypeStruct((rows, qkv.shape[1] // 2 + LANES), BF16)
    shape_up = jax.ShapeDtypeStruct((rows, up.shape[1] // 2), BF16)
    vmem = pl.BlockSpec(memory_space=pltpu.VMEM)
    vectors = [vector if vector.ndim == 2 else vector[None] for vector in vectors]
    return pl.pallas_call(
        pack_kernel,
        in_specs=[pl.BlockSpec(memory_space=pltpu.SMEM)] + [vmem] * (3 + len(vectors)),
        out_specs=[vmem] * 4,
        out_shape=[shape_qkv, shape_qkv, shape_up, shape_up],
        name="pack_weights",
    )(core.reshape(1), qkv, up, segments, *vectors)


def beside_kernel(splits, place, line, from_x, from_y, *outs):
    rows = line.shape[1]
    y, x = place[0], place[1]
    for part, py, px in ((line, y, x), (from_x, y, 1 - x), (from_y, 1 - y, x)):
        target = pl.ds(pl.multiple_of((2 * py + px) * rows, rows), rows)
        for out, (start, stop) in zip(outs, splits):
            out[target, :] = part[0, :, start:stop]


def corner_kernel(splits, place, low, high, *refs):
    outs = refs[len(refs) // 2 :]
    half = low.shape[1]
    for out, (start, stop) in zip(outs, splits):
        out[:, 0, :half, :] = low[:, :, start:stop]
        out[:, 0, half:, :] = high[:, :, start:stop]


def put_beside(place, line, from_x, from_y, splits):
    lines, rows, columns = line.shape
    part = pl.BlockSpec((1, rows, columns), lambda step, place: (step, 0, 0))
    return pl.pallas_call(
        functools.partial(beside_kernel, splits),
        grid_spec=pltpu.PrefetchScalarGridSpec(
            num_scalar_prefetch=1,
            grid=(lines,),
            in_specs=[part] * 3,
            out_specs=[
                pl.BlockSpec((4 * rows, stop - start), lambda step, place: (step, 0))
                for start, stop in splits
            ],
        ),
        out_shape=[
            jax.ShapeDtypeStruct((lines * 4 * rows, stop - start), line.dtype)
            for start, stop in splits
        ],
        cost_estimate=pl.CostEstimate(
            flops=6144 * line.size, bytes_accessed=8 * line.size, transcendentals=0
        ),
        name="put_beside",
    )(place, line, from_x, from_y)


def put_corner(place, low, high, wholes, splits):
    lines, half, columns = low.shape

    def there(step, place):
        return (0, 2 * (1 - place[0]) + 1 - place[1], 0, 0)

    part = pl.BlockSpec(low.shape, lambda step, place: (0, 0, 0))
    wholes = [whole.reshape(lines, 4, 2 * half, -1) for whole in wholes]
    return pl.pallas_call(
        functools.partial(corner_kernel, splits),
        grid_spec=pltpu.PrefetchScalarGridSpec(
            num_scalar_prefetch=1,
            grid=(1,),
            in_specs=[part] * 2 + [pl.BlockSpec(memory_space=pl.ANY)] * len(wholes),
            out_specs=[
                pl.BlockSpec((lines, 1, 2 * half, stop - start), there) for start, stop in splits
            ],
        ),
        out_shape=[jax.ShapeDtypeStruct(whole.shape, whole.dtype) for whole in wholes],
        input_output_aliases={3 + place: place for place in range(len(wholes))},
        name="put_corner",
    )(place, low, high, *wholes)


def swap_core(array):
    return lax.ppermute(array, "c", SWAP)


def take(array, place, axis=0):
    return lax.dynamic_index_in_dim(array, place, axis, keepdims=False)


def in_order(place, own, other, axis):
    first = jnp.stack([own, other], axis=axis)
    second = jnp.stack([other, own], axis=axis)
    return jnp.where(place == 0, first, second)


def over_x(array):
    count = lax.axis_size("x")
    if count != 2:
        return lax.all_to_all(array, "x", 0, 0)
    here = lax.axis_index("x")
    other = lax.ppermute(take(array, 1 - here), "x", SWAP)
    return in_order(here, take(array, here), other, 0)


def plane_split():
    return tuple(lax.axis_size(name) for name in CHIPS) == (4, 2, 2)


def after(array, *others):
    return lax.optimization_barrier((array, others))[0]


def turn_z(step):
    size = lax.axis_size("z")
    return [(place, (place + step) % size) for place in range(size)]


def gather_line(chunk):
    if not plane_split():
        return chunk
    size, z = lax.axis_size("z"), lax.axis_index("z")
    full = jnp.broadcast_to(chunk, (size,) + chunk.shape)
    for step in range(1, size):
        part = lax.ppermute(chunk, "z", turn_z(step))
        full = lax.dynamic_update_index_in_dim(full, part, (z + size - step) % size, 0)
    return full


def gather_first(line):
    if not plane_split():
        return ()
    return lax.ppermute(line, "x", SWAP), lax.ppermute(line, "y", SWAP)


def gather_second(line, came):
    if not plane_split():
        return ()
    half = line.shape[1] // 2
    from_x, from_y = came
    corner_low = lax.ppermute(from_x[:, :half], "y", SWAP)
    corner_high = lax.ppermute(from_y[:, half:], "x", SWAP)
    return corner_low, corner_high


def gather_whole(line, came, corner, *splits):
    if not plane_split():
        full = lax.all_gather(line, CHIPS).reshape(-1, line.shape[-1])
        return [full[:, start:stop] for start, stop in splits]
    place = jnp.stack([lax.axis_index("y"), lax.axis_index("x")]).astype(jnp.int32)
    wholes = put_beside(place, line, *came, splits)
    wholes = put_corner(place, *corner, wholes, splits)
    return [whole.reshape(-1, whole.shape[-1]) for whole in wholes]


def add_low(*parts):
    return functools.reduce(jnp.add, [part.astype(F32) for part in parts]).astype(BF16)


def plane_part(chunks, py, px, first, count):
    _, rows, columns = chunks.shape
    split = chunks.reshape(-1, 2, 2, rows, columns)
    size = (split.shape[0], 1, 1, count, columns)
    return lax.dynamic_slice(split, (0, py, px, first, 0), size)[:, 0, 0]


def scatter_first(chunks):
    if not plane_split():
        return ()
    half = chunks.shape[1] // 2
    y, x = lax.axis_index("y"), lax.axis_index("x")
    by_x = lax.ppermute(plane_part(chunks, 1 - y, 1 - x, 0, half), "x", SWAP)
    by_y = lax.ppermute(plane_part(chunks, 1 - y, 1 - x, half, half), "y", SWAP)
    return by_x, by_y


def scatter_second(chunks, corner):
    if not plane_split():
        return ()
    half = chunks.shape[1] // 2
    y, x = lax.axis_index("y"), lax.axis_index("x")
    to_y = jnp.concatenate(
        [
            add_low(plane_part(chunks, 1 - y, x, 0, half), corner[0]),
            plane_part(chunks, 1 - y, x, half, half),
        ],
        axis=1,
    )
    to_x = jnp.concatenate(
        [
            plane_part(chunks, y, 1 - x, 0, half),
            add_low(plane_part(chunks, y, 1 - x, half, half), corner[1]),
        ],
        axis=1,
    )
    return to_x, to_y


def scatter_send(sends):
    if not plane_split():
        return ()
    return lax.ppermute(sends[0], "x", SWAP), lax.ppermute(sends[1], "y", SWAP)


def scatter_third(chunks, came):
    y, x = lax.axis_index("y"), lax.axis_index("x")
    parts = (plane_part(chunks, y, x, 0, chunks.shape[1]),) + came
    return functools.reduce(jnp.add, [part.astype(F32) for part in parts])


def line_terms(line):
    size, z = lax.axis_size("z"), lax.axis_index("z")
    return [take(line, z)] + [
        lax.ppermute(take(line, (z + step) % size), "z", turn_z(step)) for step in range(1, size)
    ]


def add_terms(terms):
    return functools.reduce(jnp.add, [term.astype(F32) for term in terms])


def scatter_line(line):
    return add_terms(line_terms(line))


def scatter_end(chunks, came, *others):
    if not plane_split():
        return lax.psum_scatter(chunks, CHIPS, scatter_dimension=0).astype(F32)
    return scatter_line(scatter_third(chunks, came).astype(BF16), *others)


def scatter_small(terms):
    y, x = lax.axis_index("y"), lax.axis_index("x")
    terms = terms.reshape((-1, 4) + terms.shape[1:])
    line = take(terms, 2 * y + x, 1)
    for step_y, step_x in ((0, 1), (1, 0), (1, 1)):
        turn = [(place, place ^ (2 * step_y + step_x)) for place in range(4)]
        there = 2 * (y ^ step_y) + (x ^ step_x)
        line = line + lax.ppermute(take(terms, there, 1), ("y", "x"), turn)
    return line


def per_device(
    inputs,
    segments,
    cotangent,
    ln1_gain,
    ln1_shift,
    qkv_weight,
    qv_bias,
    out_weight,
    out_bias,
    ln2_gain,
    ln2_shift,
    up_weight,
    up_bias,
    down_weight,
    down_bias,
):
    _, rows, width = inputs.shape
    own_rows = out_weight.shape[0]
    own_units = down_weight.shape[0]
    chips = width // (2 * own_rows)
    core = lax.axis_index("c")
    half = width // 2
    mine = 2 * chips * own_units // 2

    seg_rows = segments.size // LANES
    in_rows = own_units % LANES == 0 and rows % LANES == 0 and own_rows >= 9 + seg_rows
    if in_rows:
        vectors = (ln1_gain, ln1_shift, qv_bias, out_bias, ln2_gain, ln2_shift, down_bias, up_bias)
        packed = pack(core, qkv_weight, up_weight, segments, vectors)
    else:
        small = jnp.concatenate(
            [ln1_gain, ln1_shift, qv_bias[0], qv_bias[1], out_bias, ln2_gain, ln2_shift, down_bias]
            + [up_bias]
        )
        small_count = small.shape[0]
        small = jnp.pad(small, (0, own_rows * LANES - small_count)).reshape(own_rows, LANES)

        def head_columns(place):
            columns = [
                lax.dynamic_slice_in_dim(qkv_weight, part * width + place * half, half, 1)
                for part in range(3)
            ]
            return jnp.concatenate(columns + [small], axis=1)

        up_split = up_weight.reshape(own_rows, chips, 2, own_units)
        packed = (
            head_columns(1 - core),
            head_columns(core),
            take(up_split, 1 - core, 2).reshape(own_rows, mine),
            take(up_split, core, 2).reshape(own_rows, mine),
        )
    send_qkv, keep_qkv, send_up, keep_up = packed
    chunk_qkv = in_order(core, keep_qkv, swap_core(send_qkv), 0).reshape(2 * own_rows, -1)
    send_up = after(send_up, chunk_qkv)
    chunk_up = in_order(core, keep_up, swap_core(send_up), 0).reshape(2 * own_rows, -1)
    chunk_out = jnp.concatenate([out_weight[:, :half], out_weight[:, half:]], axis=0)
    chunk_up = jnp.concatenate([chunk_up, chunk_out], axis=1)

    def both_cores(own):
        return jnp.concatenate([own, swap_core(own)], axis=0)

    def joined(array):
        return array.reshape((-1,) + array.shape[2:])

    line_qkv = gather_line(chunk_qkv)
    if lax.axis_size("x") == 2:
        here = lax.axis_index("x")
        other = lax.ppermute(take(inputs, 1 - here), "x", SWAP)
        own_x = in_order(here, take(inputs, here), other, 0)
    else:
        own_x = over_x(inputs)
    own_x = joined(own_x)
    total = 2 * own_x.shape[0]
    pieces = jnp.arange(total // rows, dtype=jnp.int32)
    places = jnp.where(pieces % 2 == core, 0, own_x.shape[0]) + pieces // 2 * rows

    line_up = lax.all_gather(chunk_up, "z") if plane_split() else chunk_up
    line_qkv = after(line_qkv, own_x, chunk_up)
    came_qkv = gather_first(line_qkv)
    full_x = both_cores(own_x)
    line_down, came_down = down_weight[None], ()
    if plane_split():
        line_down = after(line_down, line_qkv)
        came_down = gather_first(line_down)
    came_qkv, came_down, full_x = lax.optimization_barrier((came_qkv, came_down, full_x))
    full_x = full_x.astype(F32)
    corner_qkv = gather_second(line_qkv, came_qkv)
    plane_down = down_weight
    if plane_split():
        corner_down = gather_second(line_down, came_down)
        plane_down = gather_whole(line_down, came_down, corner_down, (0, width))[0]
    w_qkv, smalls = gather_whole(
        line_qkv, came_qkv, corner_qkv, (0, 3 * half), (3 * half, 3 * half + LANES)
    )
    smalls = smalls.reshape(2 * chips, own_rows, LANES)
    if in_rows:
        vectors = [smalls[:, place, :own_rows] for place in range(8)]
        small_up = smalls[:, 8, :own_units]
    else:
        smalls = smalls.reshape(2 * chips, -1)
        vectors = [smalls[:, place * own_rows : (place + 1) * own_rows] for place in range(8)]
        small_up = smalls[:, 8 * own_rows : 8 * own_rows + own_units]
    vectors = [vector.reshape(width).astype(F32) for vector in vectors]
    if in_rows:
        seg_all = smalls[:, 9 : 9 + seg_rows].reshape(-1, lax.axis_size("x"), 2, segments.size)
        seg_all = take(seg_all, lax.axis_index("z") * lax.axis_size("y") + lax.axis_index("y"))
        seg_all = seg_all.reshape((-1, 2) + segments.shape)
        seg_all = take(seg_all, lax.axis_index("x"), 2).reshape(-1).astype(jnp.int32)
    else:
        own_seg = over_x(segments)
        seg_all = in_order(core, own_seg, swap_core(own_seg), 1).reshape(-1)
    seg_keys = seg_all[:, None]
    seg_queries = seg_all[None, :]
    gain1, shift1, b_q, b_v, b_out, gain2, shift2, b_down = vectors
    b_up = take(small_up.reshape(chips, 2, own_units), core, 1)
    b_up = b_up.reshape(mine).astype(F32)

    normed1 = norm_forward(full_x, gain1, shift1).astype(BF16)
    normed1, line_up, plane_down = lax.optimization_barrier((normed1, line_up, plane_down))
    b_qkv = jnp.concatenate(
        [
            lax.dynamic_slice_in_dim(b_q, core * half, half),
            jnp.zeros((half,), F32),
            lax.dynamic_slice_in_dim(b_v, core * half, half),
        ]
    )
    qkv = (dot_plain(normed1, w_qkv) + b_qkv).astype(BF16)
    w_down = lax.all_gather(plane_down, "z" if plane_split() else CHIPS).reshape(mine, width)
    line_up = after(line_up, corner_qkv)
    came_up = gather_first(line_up)
    attended, logsum = attend(places, seg_keys, seg_queries, qkv)
    attended = after(attended, came_up)
    came_up = after(came_up, attended)
    corner_up = gather_second(line_up, came_up)
    w_up, all_out = gather_whole(
        line_up, came_up, corner_up, (0, mine), (mine, mine + half)
    )
    all_out = all_out.reshape(chips, 2 * own_rows, half)
    all_out = jnp.concatenate([all_out[:, :own_rows], all_out[:, own_rows:]], axis=2)
    out_keep = lax.dynamic_slice_in_dim(all_out, core * (chips // 2), chips // 2)
    out_send = lax.dynamic_slice_in_dim(all_out, (1 - core) * (chips // 2), chips // 2)
    w_out = in_order(core, out_keep, swap_core(out_send), 1).reshape(half, width)

    def add_cores(dot, left, weight):
        count = left.shape[0] // 2
        other = swap_core(dot(left[count:], weight).astype(BF16))
        return dot(left[:count], weight) + other.astype(F32)

    resid = own_x.astype(F32) + add_cores(dot_plain, attended, w_out) + b_out
    normed2_own = norm_forward(resid, gain2, shift2).astype(BF16)
    normed2 = both_cores(normed2_own)
    own_g = joined(over_x(after(cotangent, corner_up)))
    normed2, w_down, own_g = lax.optimization_barrier((normed2, w_down, own_g))
    full_g = both_cores(own_g)
    pre = dot_plain(normed2, w_up) + b_up
    active, gelu_pull = jax.vjp(gelu_tanh, pre)
    active = active.astype(BF16)
    slope = gelu_pull(jnp.ones_like(pre))[0].astype(BF16)
    active, slope = lax.optimization_barrier((active, slope))
    grad_down = dot_outer(active, full_g).astype(BF16).reshape(chips, own_units, width)
    full_g, grad_down = lax.optimization_barrier((full_g, grad_down))
    if plane_split():
        line_gd = lax.psum_scatter(
            grad_down.reshape(-1, 4, own_units, width), "z", scatter_dimension=0
        )
    else:
        line_gd = grad_down
    grad_active = dot_back(full_g, w_down)
    grad_pre = (grad_active * slope.astype(F32)).astype(BF16)
    mixed = add_cores(dot_plain, after(active, grad_pre), w_down) + b_down
    outputs = (resid + mixed).astype(BF16).reshape(-1, rows, width)
    up_terms = dot_outer(normed2, grad_pre).astype(BF16).reshape(chips, 2 * own_rows, mine)
    grad_pre, up_terms = lax.optimization_barrier((grad_pre, up_terms))
    corner_gu = scatter_first(up_terms)
    grad_normed2 = add_cores(dot_back, grad_pre, w_up)
    corner_gu, grad_normed2 = lax.optimization_barrier((corner_gu, grad_normed2))
    own_g32 = own_g.astype(F32)
    _, norm2_pull = jax.vjp(norm_forward, resid, gain2, shift2)
    grad_part, grad_gain2, grad_shift2 = norm2_pull(grad_normed2)
    grad_resid = own_g32 + grad_part

    grad_branch_own = grad_resid.astype(BF16)
    sends_gu = scatter_second(up_terms, corner_gu)
    grad_branch_own, sends_gu = lax.optimization_barrier((grad_branch_own, sends_gu))
    came_gu = scatter_send(sends_gu)
    grad_branch = both_cores(grad_branch_own)
    grad_attended = dot_back(grad_branch, w_out).astype(BF16)
    grad_out = dot_outer(attended, grad_branch).astype(BF16)
    grad_out = grad_out.reshape(chips // 2, 2, own_rows, width)
    out_other = swap_core(take(grad_out, 1 - core, 1))
    out_terms = in_order(core, take(grad_out, core, 1), out_other, 0)
    out_terms = out_terms.reshape(chips, own_rows, width)
    out_terms = jnp.concatenate([out_terms[..., :half], out_terms[..., half:]], axis=1)
    if plane_split():
        line_gu = scatter_third(up_terms, came_gu).astype(BF16)
    else:
        line_gu = up_terms

    pairs = half // PAIR
    few = pairs // 2
    grad_low = attend_back(places, seg_keys, seg_queries, qkv, grad_attended, logsum, 0, few)
    low_terms = dot_outer(normed1, grad_low).astype(BF16).reshape(chips, 2 * own_rows, -1)
    low_terms = jnp.concatenate([low_terms, out_terms], axis=2)
    grad_attended, low_terms, outputs, line_gu = lax.optimization_barrier(
        (grad_attended, low_terms, outputs, line_gu)
    )
    up_got = line_terms(line_gu) if plane_split() else []
    corner_low = scatter_first(low_terms)
    grad_high = attend_back(
        places, seg_keys, seg_queries, qkv, grad_attended, logsum, few, pairs - few
    )
    corner_low, grad_high, up_got, line_gd = lax.optimization_barrier(
        (corner_low, grad_high, up_got, line_gd)
    )
    if plane_split():
        down_grad = lax.psum_scatter(line_gd, ("y", "x"), scatter_dimension=0).astype(F32)
    else:
        down_grad = lax.psum_scatter(line_gd, CHIPS, scatter_dimension=0).astype(F32)
    up_sum = add_terms(up_got) if plane_split() else scatter_end(line_gu, ())
    sends_low = scatter_second(low_terms, corner_low)
    grad_high, sends_low = lax.optimization_barrier((grad_high, sends_low))
    high_terms = dot_outer(normed1, grad_high).astype(BF16).reshape(chips, 2 * own_rows, -1)
    came_low = scatter_send(sends_low)
    corner_high = scatter_first(high_terms)

    low_width, high_width = few * PAIR, (pairs - few) * PAIR
    w_low = jnp.concatenate(
        [w_qkv[:, part * half : part * half + low_width] for part in range(3)], axis=1
    )
    w_high = jnp.concatenate(
        [w_qkv[:, part * half + low_width : (part + 1) * half] for part in range(3)], axis=1
    )
    count = grad_low.shape[0] // 2
    other = dot_back(grad_low[count:], w_low) + dot_back(grad_high[count:], w_high)
    other = swap_core(other.astype(BF16)).astype(F32)
    grad_normed1 = dot_back(grad_low[:count], w_low) + dot_back(grad_high[:count], w_high) + other
    own_x32 = own_x.astype(F32)
    _, norm1_pull = jax.vjp(norm_forward, own_x32, gain1, shift1)
    grad_part1, grad_gain1, grad_shift1 = norm1_pull(grad_normed1)
    grad_x = (grad_resid + grad_part1).reshape(-1, rows, width)

    def place_heads(sums):
        zeros = jnp.zeros((width,), F32)
        return lax.dynamic_update_slice_in_dim(zeros, sums, core * half, 0)

    low_sums = jnp.sum(grad_low.astype(F32), axis=0)
    high_sums = jnp.sum(grad_high.astype(F32), axis=0)

    def head_sums(part):
        low = low_sums[part * low_width : (part + 1) * low_width]
        high = high_sums[part * high_width : (part + 1) * high_width]
        return place_heads(jnp.concatenate([low, high]))

    small_sums = [
        grad_gain1,
        grad_shift1,
        head_sums(0),
        head_sums(2),
        jnp.sum(grad_branch_own.astype(F32), axis=0),
        grad_gain2,
        grad_shift2,
        jnp.sum(own_g32, axis=0),
    ]
    up_sums = jnp.sum(grad_pre.astype(F32), axis=0)
    small_terms = jnp.concatenate(
        [vector.reshape(chips, 2 * own_rows) for vector in small_sums]
        + [up_sums.reshape(chips, own_units)],
        axis=1,
    )
    small_width = small_terms.shape[1]
    small_terms = jnp.pad(small_terms, ((0, 0), (0, 2 * own_rows * LANES - small_width)))
    small_terms = small_terms.reshape(chips, 2 * own_rows, LANES)

    corner_high, came_low, grad_x, small_terms = lax.optimization_barrier(
        (corner_high, came_low, grad_x, small_terms)
    )
    sends_high = scatter_second(high_terms, corner_high)
    came_high = scatter_send(sends_high)

    count = lax.axis_size("x")
    if count == 2:
        here = lax.axis_index("x")
        other = lax.ppermute(take(grad_x, 1 - here).astype(BF16), "x", SWAP).astype(F32)
        input_grad = in_order(here, take(grad_x, here), other, 0)
    else:
        input_grad = over_x(grad_x)
    if plane_split():
        line_low = scatter_third(low_terms, came_low)
        low_sum = scatter_line(line_low.astype(BF16))
        line_high = scatter_third(high_terms, came_high)
        line_high = jnp.concatenate([line_high, scatter_small(small_terms)], axis=2).astype(BF16)
        line_high, low_sum, input_grad, down_grad = lax.optimization_barrier(
            (line_high, low_sum, input_grad, down_grad)
        )
        outputs = over_x(after(outputs, came_high))
        high_sum = scatter_line(line_high)
    else:
        low_sum = scatter_end(low_terms, ())
        outputs = over_x(outputs)
        high_sum = scatter_end(jnp.concatenate([high_terms.astype(F32), small_terms], axis=2), ())
    out_sum = low_sum[:, 3 * low_width :]
    qkv_sum = jnp.concatenate(
        [
            piece
            for part in range(3)
            for piece in (
                low_sum[:, part * low_width : (part + 1) * low_width],
                high_sum[:, part * high_width : (part + 1) * high_width],
            )
        ],
        axis=1,
    )
    sums = high_sum[:, 3 * high_width :].reshape(-1)
    up_sum = up_sum.reshape(2, own_rows, mine)
    out_grad = jnp.concatenate([out_sum[:own_rows], out_sum[own_rows:]], axis=1)
    up_other = swap_core(take(up_sum, 1 - core))
    up_grad = in_order(
        core,
        take(up_sum, core).reshape(own_rows, chips, own_units),
        up_other.reshape(own_rows, chips, own_units),
        2,
    )
    up_grad = up_grad.reshape(own_rows, 2 * mine)
    weight_sum = qkv_sum.reshape(2, own_rows, 3 * half)
    qkv_other = swap_core(take(weight_sum, 1 - core))
    qkv_grad = in_order(
        core,
        take(weight_sum, core).reshape(own_rows, 3, half),
        qkv_other.reshape(own_rows, 3, half),
        2,
    )
    qkv_grad = qkv_grad.reshape(own_rows, 6 * half)
    shared = sums[: 16 * own_rows].reshape(8, 2, own_rows)
    shared = take(shared, core, 1) + swap_core(take(shared, 1 - core, 1))
    up_bias_grad = sums[16 * own_rows : 16 * own_rows + own_units]

    return (
        outputs,
        input_grad,
        shared[0],
        shared[1],
        qkv_grad,
        shared[2:4],
        out_grad,
        shared[4],
        shared[5],
        shared[6],
        up_grad,
        up_bias_grad,
        down_grad,
        shared[7],
    )


def solution(mesh):
    groups, members = mesh.devices.shape
    split = Mesh(mesh.devices.reshape(groups // 2, 2, members // 2, 2), ("z", "y", "x", "c"))
    every = ("z", "y", "x", "c")
    tokens = P(("z", "y"), ("x", "c"), None)
    vector = P(every)
    matrix = P(every, None)
    return jax.shard_map(
        per_device,
        mesh=split,
        in_specs=(
            tokens,
            P(("z", "y"), ("x", "c")),
            tokens,
            vector,
            vector,
            matrix,
            P(None, every),
            matrix,
            vector,
            vector,
            vector,
            matrix,
            vector,
            matrix,
            vector,
        ),
        out_specs=(
            tokens,
            tokens,
            vector,
            vector,
            matrix,
            P(None, every),
            matrix,
            vector,
            vector,
            vector,
            matrix,
            vector,
            matrix,
            vector,
        ),
        check_vma=False,
    )
```

```python
import functools

import jax
import jax.numpy as jnp
from jax import lax
from jax.experimental import pallas as pl
from jax.experimental.pallas import tpu as pltpu
from jax.sharding import Mesh
from jax.sharding import PartitionSpec as P

HEAD_DIM = 64
PAIR = 2 * HEAD_DIM
LANES = 128
BLOCK = 256
SWAP = [(0, 1), (1, 0)]
CHIPS = ("z", "y", "x")
BF16 = jnp.bfloat16
F32 = jnp.float32


def norm_forward(values, gain, shift):
    average = jnp.mean(values, axis=-1, keepdims=True)
    centred = values - average
    spread = jnp.mean(centred * centred, axis=-1, keepdims=True)
    return centred * lax.rsqrt(spread + 1e-05) * gain + shift


def gelu_tanh(values):
    return jax.nn.gelu(values, approximate=True)


def dot_plain(left, right):
    return jnp.dot(left, right, preferred_element_type=F32)


def dot_outer(left, right):
    return lax.dot_general(left, right, (((0,), (0,)), ((), ())), preferred_element_type=F32)


def dot_back(left, weight):
    return lax.dot_general(left, weight, (((1,), (1,)), ((), ())), preferred_element_type=F32)


def fill_bias(seg_keys, seg_queries, bias):
    total = bias.shape[0]
    for start in range(0, total, BLOCK):
        stop = start + BLOCK
        places_k = lax.broadcasted_iota(jnp.int32, (stop, BLOCK), 0)
        places_q = lax.broadcasted_iota(jnp.int32, (stop, BLOCK), 1) + start
        kept = (seg_keys[:stop, :] == seg_queries[:, start:stop]) & (places_k <= places_q)
        bias[:stop, start:stop] = jnp.where(kept, 0.0, -1000000000.0)


def piece_rows(places, first, piece):
    return pl.ds(pl.multiple_of(places[first // piece], piece), piece)


def load_rows(places, source, first, count, columns):
    piece = source.shape[0] // places.shape[0]
    return jnp.concatenate(
        [
            source[piece_rows(places, start, piece), columns]
            for start in range(first, first + count, piece)
        ],
        axis=0,
    )


def store_rows(places, target, first, count, columns, rows):
    piece = target.shape[0] // places.shape[0]
    for start in range(0, count, piece):
        target[piece_rows(places, first + start, piece), columns] = rows[start : start + piece]


def head_masks():
    lanes = lax.broadcasted_iota(jnp.int32, (1, PAIR), 1)
    return [(lanes // HEAD_DIM == head).astype(F32).astype(BF16) for head in range(2)]


def turned(values):
    return values.astype(F32).T.astype(BF16)


def forward_kernel(places, seg_keys, seg_queries, qkv, out, logsum, bias):
    step = pl.program_id(0)
    total = out.shape[0]
    width = out.shape[1]

    @pl.when(step == 0)
    def _():
        fill_bias(seg_keys, seg_queries, bias)

    column = pl.multiple_of(step * PAIR, PAIR)
    here = pl.ds(column, PAIR)
    keys = load_rows(places, qkv, 0, total, pl.ds(width + column, PAIR))
    values_t = turned(load_rows(places, qkv, 0, total, pl.ds(2 * width + column, PAIR)))
    masks = head_masks()
    for start in range(0, total, BLOCK):
        stop = start + BLOCK
        queries = load_rows(places, qkv, start, BLOCK, here)
        queries = queries * jnp.asarray(HEAD_DIM ** (-0.5), BF16)
        parts = []
        for head in range(2):
            scores = dot_back(keys[:stop], queries * masks[head]) + bias[:stop, start:stop]
            highest = jnp.max(scores, axis=0, keepdims=True)
            expon = jnp.exp(scores - highest)
            totals = jnp.sum(expon, axis=0, keepdims=True)
            first = head * HEAD_DIM
            part = dot_plain(values_t[first : first + HEAD_DIM, :stop], expon.astype(BF16))
            parts.append(part / totals)
            logsum[0, head : head + 1, start:stop] = highest + jnp.log(totals)
        rows = jnp.concatenate(parts, axis=0).T.astype(BF16)
        store_rows(places, out, start, BLOCK, here, rows)


def backward_kernel(
    first_pair, places, seg_keys, seg_queries, qkv, grad, logsum, grad_qkv, bias, sum_k, sum_v
):
    step = pl.program_id(0)
    total, width = grad.shape

    @pl.when(step == 0)
    def _():
        fill_bias(seg_keys, seg_queries, bias)

    column = pl.multiple_of((first_pair + step) * PAIR, PAIR)
    here = pl.ds(column, PAIR)
    here_k = pl.ds(width + column, PAIR)
    here_v = pl.ds(2 * width + column, PAIR)
    part_width = grad_qkv.shape[1] // 3
    part_column = pl.multiple_of(step * PAIR, PAIR)
    put_q = pl.ds(part_column, PAIR)
    put_k = pl.ds(part_width + part_column, PAIR)
    put_v = pl.ds(2 * part_width + part_column, PAIR)
    keys = load_rows(places, qkv, 0, total, here_k)
    values = load_rows(places, qkv, 0, total, here_v)
    keys_t = turned(keys)
    masks = head_masks()
    sum_k[...] = jnp.zeros_like(sum_k)
    sum_v[...] = jnp.zeros_like(sum_v)
    for start in range(0, total, BLOCK):
        stop = start + BLOCK
        queries = load_rows(places, qkv, start, BLOCK, here)
        queries = queries * jnp.asarray(HEAD_DIM ** (-0.5), BF16)
        grads = load_rows(places, grad, start, BLOCK, here)
        parts = []
        for head in range(2):
            query = queries * masks[head]
            grad_head = grads * masks[head]
            scores = dot_back(keys[:stop], query) + bias[:stop, start:stop]
            weights = jnp.exp(scores - logsum[0, head : head + 1, start:stop])
            grad_weights = dot_back(values[:stop], grad_head)
            inner = jnp.sum(weights * grad_weights, axis=0, keepdims=True)
            grad_scores = (weights * (grad_weights - inner)).astype(BF16)
            sum_v[:stop, :] += dot_plain(weights.astype(BF16), grad_head)
            sum_k[:stop, :] += dot_plain(grad_scores, query)
            first = head * HEAD_DIM
            parts.append(dot_plain(keys_t[first : first + HEAD_DIM, :stop], grad_scores))
        grad_queries = jnp.concatenate(parts, axis=0).T * HEAD_DIM ** (-0.5)
        store_rows(places, grad_qkv, start, BLOCK, put_q, grad_queries.astype(BF16))
    store_rows(places, grad_qkv, 0, total, put_k, sum_k[...].astype(BF16))
    store_rows(places, grad_qkv, 0, total, put_v, sum_v[...].astype(BF16))


def whole_block(shape):
    return pl.BlockSpec(shape, lambda step: (0,) * len(shape))


def attend(places, seg_keys, seg_queries, qkv):
    total, width3 = qkv.shape
    width = width3 // 3
    pairs = width // PAIR
    return pl.pallas_call(
        forward_kernel,
        grid=(pairs,),
        in_specs=[
            pl.BlockSpec(memory_space=pltpu.SMEM),
            whole_block((total, 1)),
            whole_block((1, total)),
            whole_block((total, width3)),
        ],
        out_specs=[
            whole_block((total, width)),
            pl.BlockSpec((1, 2, total), lambda step: (step, 0, 0)),
        ],
        out_shape=[
            jax.ShapeDtypeStruct((total, width), BF16),
            jax.ShapeDtypeStruct((pairs, 2, total), F32),
        ],
        scratch_shapes=[pltpu.VMEM((total, total), F32)],
        compiler_params=pltpu.CompilerParams(vmem_limit_bytes=48 * 1024 * 1024),
        cost_estimate=pl.CostEstimate(
            flops=40 * total * total * width, bytes_accessed=total * width, transcendentals=0
        ),
        name="attention_forward",
    )(places, seg_keys, seg_queries, qkv)


def attend_back(places, seg_keys, seg_queries, qkv, grad, logsum, first, pairs):
    total, width = grad.shape
    return pl.pallas_call(
        functools.partial(backward_kernel, first),
        grid=(pairs,),
        in_specs=[
            pl.BlockSpec(memory_space=pltpu.SMEM),
            whole_block((total, 1)),
            whole_block((1, total)),
            whole_block((total, 3 * width)),
            whole_block((total, width)),
            pl.BlockSpec((1, 2, total), lambda step: (first + step, 0, 0)),
        ],
        out_specs=whole_block((total, 3 * pairs * PAIR)),
        out_shape=jax.ShapeDtypeStruct((total, 3 * pairs * PAIR), BF16),
        scratch_shapes=[
            pltpu.VMEM((total, total), F32),
            pltpu.VMEM((total, PAIR), F32),
            pltpu.VMEM((total, PAIR), F32),
        ],
        compiler_params=pltpu.CompilerParams(vmem_limit_bytes=48 * 1024 * 1024),
        cost_estimate=pl.CostEstimate(
            flops=total * total, bytes_accessed=total * width, transcendentals=0
        ),
        name="attention_backward",
    )(places, seg_keys, seg_queries, qkv, grad, logsum)


def pack_kernel(core, qkv, up, segments, *refs):
    vectors, (send_qkv, keep_qkv, send_up, keep_up) = refs[:-4], refs[-4:]
    rows, width3 = qkv.shape
    half = width3 // 6
    blocks = up.shape[1] // (2 * LANES)
    for place, to_qkv, to_up in ((1 - core[0], send_qkv, send_up), (core[0], keep_qkv, keep_up)):
        for part in range(3):
            start = pl.multiple_of(2 * part * half + place * half, half)
            to_qkv[:, part * half : (part + 1) * half] = qkv[:, pl.ds(start, half)]
        to_qkv[:, 3 * half :] = jnp.zeros((rows, LANES), BF16)
        row = 0
        for vector in vectors:
            count, size = vector.shape
            to_qkv[row : row + count, 3 * half : 3 * half + size] = vector[...]
            row += count
        for sequence in range(segments.shape[0]):
            for start in range(0, segments.shape[1], LANES):
                numbers = segments[sequence : sequence + 1, start : start + LANES]
                to_qkv[row : row + 1, 3 * half :] = numbers.astype(F32).astype(BF16)
                row += 1
        for block in range(blocks):
            start = pl.multiple_of((2 * block + place) * LANES, LANES)
            to_up[:, block * LANES : (block + 1) * LANES] = up[:, pl.ds(start, LANES)]


def pack(core, qkv, up, segments, vectors):
    rows = qkv.shape[0]
    shape_qkv = jax.ShapeDtypeStruct((rows, qkv.shape[1] // 2 + LANES), BF16)
    shape_up = jax.ShapeDtypeStruct((rows, up.shape[1] // 2), BF16)
    vmem = pl.BlockSpec(memory_space=pltpu.VMEM)
    vectors = [vector if vector.ndim == 2 else vector[None] for vector in vectors]
    return pl.pallas_call(
        pack_kernel,
        in_specs=[pl.BlockSpec(memory_space=pltpu.SMEM)] + [vmem] * (3 + len(vectors)),
        out_specs=[vmem] * 4,
        out_shape=[shape_qkv, shape_qkv, shape_up, shape_up],
        name="pack_weights",
    )(core.reshape(1), qkv, up, segments, *vectors)


def beside_kernel(splits, place, line, from_x, from_y, *outs):
    rows = line.shape[1]
    y, x = place[0], place[1]
    for part, py, px in ((line, y, x), (from_x, y, 1 - x), (from_y, 1 - y, x)):
        target = pl.ds(pl.multiple_of((2 * py + px) * rows, rows), rows)
        for out, (start, stop) in zip(outs, splits):
            out[target, :] = part[0, :, start:stop]


def corner_kernel(splits, place, low, high, *refs):
    outs = refs[len(refs) // 2 :]
    half = low.shape[1]
    for out, (start, stop) in zip(outs, splits):
        out[:, 0, :half, :] = low[:, :, start:stop]
        out[:, 0, half:, :] = high[:, :, start:stop]


def put_beside(place, line, from_x, from_y, splits):
    lines, rows, columns = line.shape
    part = pl.BlockSpec((1, rows, columns), lambda step, place: (step, 0, 0))
    return pl.pallas_call(
        functools.partial(beside_kernel, splits),
        grid_spec=pltpu.PrefetchScalarGridSpec(
            num_scalar_prefetch=1,
            grid=(lines,),
            in_specs=[part] * 3,
            out_specs=[
                pl.BlockSpec((4 * rows, stop - start), lambda step, place: (step, 0))
                for start, stop in splits
            ],
        ),
        out_shape=[
            jax.ShapeDtypeStruct((lines * 4 * rows, stop - start), line.dtype)
            for start, stop in splits
        ],
        cost_estimate=pl.CostEstimate(
            flops=6144 * line.size, bytes_accessed=8 * line.size, transcendentals=0
        ),
        name="put_beside",
    )(place, line, from_x, from_y)


def put_corner(place, low, high, wholes, splits):
    lines, half, columns = low.shape

    def there(step, place):
        return (0, 2 * (1 - place[0]) + 1 - place[1], 0, 0)

    part = pl.BlockSpec(low.shape, lambda step, place: (0, 0, 0))
    wholes = [whole.reshape(lines, 4, 2 * half, -1) for whole in wholes]
    return pl.pallas_call(
        functools.partial(corner_kernel, splits),
        grid_spec=pltpu.PrefetchScalarGridSpec(
            num_scalar_prefetch=1,
            grid=(1,),
            in_specs=[part] * 2 + [pl.BlockSpec(memory_space=pl.ANY)] * len(wholes),
            out_specs=[
                pl.BlockSpec((lines, 1, 2 * half, stop - start), there) for start, stop in splits
            ],
        ),
        out_shape=[jax.ShapeDtypeStruct(whole.shape, whole.dtype) for whole in wholes],
        input_output_aliases={3 + place: place for place in range(len(wholes))},
        name="put_corner",
    )(place, low, high, *wholes)


def join_kernel(first, second, out):
    count = first.shape[0]
    out[:count] = first[...]
    out[count:] = second[...]


def join(first, second):
    count, columns = first.shape
    half = pl.BlockSpec((count, columns // 2), lambda step: (0, step))
    return pl.pallas_call(
        join_kernel,
        grid=(2,),
        in_specs=[half, half],
        out_specs=pl.BlockSpec((2 * count, columns // 2), lambda step: (0, step)),
        out_shape=jax.ShapeDtypeStruct((2 * count, columns), first.dtype),
        name="join",
    )(first, second)


def swap_core(array):
    return lax.ppermute(array, "c", SWAP)


def take(array, place, axis=0):
    return lax.dynamic_index_in_dim(array, place, axis, keepdims=False)


def in_order(place, own, other, axis):
    first = jnp.stack([own, other], axis=axis)
    second = jnp.stack([other, own], axis=axis)
    return jnp.where(place == 0, first, second)


def over_x(array):
    count = lax.axis_size("x")
    if count != 2:
        return lax.all_to_all(array, "x", 0, 0)
    here = lax.axis_index("x")
    other = lax.ppermute(take(array, 1 - here), "x", SWAP)
    return in_order(here, take(array, here), other, 0)


def plane_split():
    return tuple(lax.axis_size(name) for name in CHIPS) == (4, 2, 2)


def after(array, *others):
    return lax.optimization_barrier((array, others))[0]


def turn_z(step):
    size = lax.axis_size("z")
    return [(place, (place + step) % size) for place in range(size)]


def gather_line(chunk):
    if not plane_split():
        return chunk
    size, z = lax.axis_size("z"), lax.axis_index("z")
    full = jnp.broadcast_to(chunk, (size,) + chunk.shape)
    for step in range(1, size):
        part = lax.ppermute(chunk, "z", turn_z(step))
        full = lax.dynamic_update_index_in_dim(full, part, (z + size - step) % size, 0)
    return full


def gather_first(line):
    if not plane_split():
        return ()
    return lax.ppermute(line, "x", SWAP), lax.ppermute(line, "y", SWAP)


def gather_second(line, came):
    if not plane_split():
        return ()
    half = line.shape[1] // 2
    from_x, from_y = came
    corner_low = lax.ppermute(from_x[:, :half], "y", SWAP)
    corner_high = lax.ppermute(from_y[:, half:], "x", SWAP)
    return corner_low, corner_high


def gather_whole(line, came, corner, *splits):
    if not plane_split():
        full = lax.all_gather(line, CHIPS).reshape(-1, line.shape[-1])
        return [full[:, start:stop] for start, stop in splits]
    place = jnp.stack([lax.axis_index("y"), lax.axis_index("x")]).astype(jnp.int32)
    wholes = put_beside(place, line, *came, splits)
    wholes = put_corner(place, *corner, wholes, splits)
    return [whole.reshape(-1, whole.shape[-1]) for whole in wholes]


def add_low(*parts):
    return functools.reduce(jnp.add, [part.astype(F32) for part in parts]).astype(BF16)


def plane_turns():
    for step_y, step_x in ((0, 1), (1, 0), (1, 1)):
        turn = [(place, place ^ (2 * step_y + step_x)) for place in range(4)]
        yield step_y, step_x, turn


def plane_part(chunks, step_y, step_x):
    y, x = lax.axis_index("y"), lax.axis_index("x")
    split = chunks.reshape((-1, 4) + chunks.shape[1:])
    return take(split, 2 * (y ^ step_y) + (x ^ step_x), 1)


def scatter_first(chunks):
    if not plane_split():
        return []
    return [
        lax.ppermute(plane_part(chunks, step_y, step_x), ("y", "x"), turn)
        for step_y, step_x, turn in plane_turns()
    ]


def scatter_third(chunks, came):
    return add_terms([plane_part(chunks, 0, 0)] + list(came))


def line_terms(line):
    size, z = lax.axis_size("z"), lax.axis_index("z")
    return [take(line, z)] + [
        lax.ppermute(take(line, (z + step) % size), "z", turn_z(step)) for step in range(1, size)
    ]


def add_terms(terms):
    return functools.reduce(jnp.add, [term.astype(F32) for term in terms])


def scatter_line(line):
    return add_terms(line_terms(line))


def scatter_end(chunks, came, *others):
    if not plane_split():
        return lax.psum_scatter(chunks, CHIPS, scatter_dimension=0).astype(F32)
    return scatter_line(scatter_third(chunks, came).astype(BF16), *others)


def scatter_small(terms):
    return scatter_third(terms, scatter_first(terms))


def per_device(
    inputs,
    segments,
    cotangent,
    ln1_gain,
    ln1_shift,
    qkv_weight,
    qv_bias,
    out_weight,
    out_bias,
    ln2_gain,
    ln2_shift,
    up_weight,
    up_bias,
    down_weight,
    down_bias,
):
    _, rows, width = inputs.shape
    own_rows = out_weight.shape[0]
    own_units = down_weight.shape[0]
    chips = width // (2 * own_rows)
    core = lax.axis_index("c")
    half = width // 2
    mine = 2 * chips * own_units // 2

    seg_rows = segments.size // LANES
    in_rows = own_units % LANES == 0 and rows % LANES == 0 and own_rows >= 9 + seg_rows
    if in_rows:
        vectors = (ln1_gain, ln1_shift, qv_bias, out_bias, ln2_gain, ln2_shift, down_bias, up_bias)
        packed = pack(core, qkv_weight, up_weight, segments, vectors)
    else:
        small = jnp.concatenate(
            [ln1_gain, ln1_shift, qv_bias[0], qv_bias[1], out_bias, ln2_gain, ln2_shift, down_bias]
            + [up_bias]
        )
        small_count = small.shape[0]
        small = jnp.pad(small, (0, own_rows * LANES - small_count)).reshape(own_rows, LANES)

        def head_columns(place):
            columns = [
                lax.dynamic_slice_in_dim(qkv_weight, part * width + place * half, half, 1)
                for part in range(3)
            ]
            return jnp.concatenate(columns + [small], axis=1)

        up_split = up_weight.reshape(own_rows, chips, 2, own_units)
        packed = (
            head_columns(1 - core),
            head_columns(core),
            take(up_split, 1 - core, 2).reshape(own_rows, mine),
            take(up_split, core, 2).reshape(own_rows, mine),
        )
    send_qkv, keep_qkv, send_up, keep_up = packed
    chunk_qkv = in_order(core, keep_qkv, swap_core(send_qkv), 0).reshape(2 * own_rows, -1)
    send_up = after(send_up, chunk_qkv)
    chunk_up = in_order(core, keep_up, swap_core(send_up), 0).reshape(2 * own_rows, -1)
    chunk_out = jnp.concatenate([out_weight[:, :half], out_weight[:, half:]], axis=0)
    chunk_up = jnp.concatenate([chunk_up, chunk_out], axis=1)

    def both_cores(own):
        return join(own, swap_core(own))

    def joined(array):
        return array.reshape((-1,) + array.shape[2:])

    line_qkv = gather_line(chunk_qkv)
    if lax.axis_size("x") == 2:
        here = lax.axis_index("x")
        other = lax.ppermute(take(inputs, 1 - here), "x", SWAP)
        own_x = in_order(here, take(inputs, here), other, 0)
    else:
        own_x = over_x(inputs)
    own_x = joined(own_x)
    total = 2 * own_x.shape[0]
    pieces = jnp.arange(total // rows, dtype=jnp.int32)
    places = jnp.where(pieces % 2 == core, 0, own_x.shape[0]) + pieces // 2 * rows

    line_up = lax.all_gather(chunk_up, "z") if plane_split() else chunk_up
    line_qkv = after(line_qkv, own_x, chunk_up)
    came_qkv = gather_first(line_qkv)
    full_x = both_cores(own_x)
    line_down, came_down = down_weight[None], ()
    if plane_split():
        line_down = after(line_down, came_qkv)
        came_down = gather_first(line_down)
    full_x = full_x.astype(F32)
    corner_qkv = gather_second(line_qkv, came_qkv)
    plane_down = down_weight
    if plane_split():
        corner_down = gather_second(line_down, came_down)
        plane_down = gather_whole(line_down, came_down, corner_down, (0, width))[0]
    w_qkv, smalls = gather_whole(
        line_qkv, came_qkv, corner_qkv, (0, 3 * half), (3 * half, 3 * half + LANES)
    )
    smalls = smalls.reshape(2 * chips, own_rows, LANES)
    if in_rows:
        vectors = [smalls[:, place, :own_rows] for place in range(8)]
        small_up = smalls[:, 8, :own_units]
    else:
        smalls = smalls.reshape(2 * chips, -1)
        vectors = [smalls[:, place * own_rows : (place + 1) * own_rows] for place in range(8)]
        small_up = smalls[:, 8 * own_rows : 8 * own_rows + own_units]
    vectors = [vector.reshape(width).astype(F32) for vector in vectors]
    if in_rows:
        seg_all = smalls[:, 9 : 9 + seg_rows].reshape(-1, lax.axis_size("x"), 2, segments.size)
        seg_all = take(seg_all, lax.axis_index("z") * lax.axis_size("y") + lax.axis_index("y"))
        seg_all = seg_all.reshape((-1, 2) + segments.shape)
        seg_all = take(seg_all, lax.axis_index("x"), 2).reshape(-1).astype(jnp.int32)
    else:
        own_seg = over_x(segments)
        seg_all = in_order(core, own_seg, swap_core(own_seg), 1).reshape(-1)
    seg_keys = seg_all[:, None]
    seg_queries = seg_all[None, :]
    gain1, shift1, b_q, b_v, b_out, gain2, shift2, b_down = vectors
    b_up = take(small_up.reshape(chips, 2, own_units), core, 1)
    b_up = b_up.reshape(mine).astype(F32)

    normed1 = norm_forward(full_x, gain1, shift1).astype(BF16)
    normed1, line_up, plane_down = lax.optimization_barrier((normed1, line_up, plane_down))
    b_qkv = jnp.concatenate(
        [
            lax.dynamic_slice_in_dim(b_q, core * half, half),
            jnp.zeros((half,), F32),
            lax.dynamic_slice_in_dim(b_v, core * half, half),
        ]
    )
    qkv = (dot_plain(normed1, w_qkv) + b_qkv).astype(BF16)
    w_down = lax.all_gather(plane_down, "z" if plane_split() else CHIPS).reshape(mine, width)
    line_up = after(line_up, corner_qkv)
    came_up = gather_first(line_up)
    attended, logsum = attend(places, seg_keys, seg_queries, qkv)
    attended = after(attended, came_up)
    came_up = after(came_up, attended)
    corner_up = gather_second(line_up, came_up)
    w_up, all_out = gather_whole(
        line_up, came_up, corner_up, (0, mine), (mine, mine + half)
    )
    all_out = all_out.reshape(chips, 2 * own_rows, half)
    all_out = jnp.concatenate([all_out[:, :own_rows], all_out[:, own_rows:]], axis=2)
    out_keep = lax.dynamic_slice_in_dim(all_out, core * (chips // 2), chips // 2)
    out_send = lax.dynamic_slice_in_dim(all_out, (1 - core) * (chips // 2), chips // 2)
    w_out = in_order(core, out_keep, swap_core(out_send), 1).reshape(half, width)

    def add_cores(dot, left, weight):
        count = left.shape[0] // 2
        other = swap_core(dot(left[count:], weight).astype(BF16))
        return dot(left[:count], weight) + other.astype(F32)

    own_g = joined(over_x(after(cotangent, came_up)))
    attended, own_g = lax.optimization_barrier((attended, own_g))
    resid = own_x.astype(F32) + add_cores(dot_plain, attended, w_out) + b_out
    normed2_own = norm_forward(resid, gain2, shift2).astype(BF16)
    normed2 = both_cores(normed2_own)
    normed2, w_down = lax.optimization_barrier((normed2, w_down))
    full_g = both_cores(own_g)
    pre = dot_plain(normed2, w_up) + b_up
    active, gelu_pull = jax.vjp(gelu_tanh, pre)
    active = active.astype(BF16)
    slope = gelu_pull(jnp.ones_like(pre))[0].astype(BF16)
    active, slope = lax.optimization_barrier((active, slope))
    grad_down = dot_outer(active, full_g).astype(BF16).reshape(chips, own_units, width)
    full_g, grad_down = lax.optimization_barrier((full_g, grad_down))
    if plane_split():
        line_gd = lax.psum_scatter(
            grad_down.reshape(-1, 4, own_units, width), "z", scatter_dimension=0
        )
    else:
        line_gd = grad_down
    grad_active = dot_back(full_g, w_down)
    grad_pre = (grad_active * slope.astype(F32)).astype(BF16)
    up_terms = dot_outer(normed2, grad_pre).astype(BF16).reshape(chips, 2 * own_rows, mine)
    grad_pre, up_terms = lax.optimization_barrier((grad_pre, up_terms))
    came_gu = scatter_first(up_terms)
    grad_normed2 = add_cores(dot_back, grad_pre, w_up)
    own_g32 = own_g.astype(F32)
    _, norm2_pull = jax.vjp(norm_forward, resid, gain2, shift2)
    grad_part, grad_gain2, grad_shift2 = norm2_pull(grad_normed2)
    grad_resid = own_g32 + grad_part

    grad_branch_own = grad_resid.astype(BF16)
    grad_branch = both_cores(grad_branch_own)
    grad_attended = dot_back(grad_branch, w_out).astype(BF16)
    grad_out = dot_outer(attended, grad_branch).astype(BF16)
    grad_out = grad_out.reshape(chips // 2, 2, own_rows, width)
    out_other = swap_core(take(grad_out, 1 - core, 1))
    out_terms = in_order(core, take(grad_out, core, 1), out_other, 0)
    out_terms = out_terms.reshape(chips, own_rows, width)
    out_terms = jnp.concatenate([out_terms[..., :half], out_terms[..., half:]], axis=1)
    pairs = half // PAIR
    few = pairs // 2
    grad_low = attend_back(places, seg_keys, seg_queries, qkv, grad_attended, logsum, 0, few)
    low_terms = dot_outer(normed1, grad_low).astype(BF16).reshape(chips, 2 * own_rows, -1)
    low_terms = jnp.concatenate([low_terms, out_terms], axis=2)
    grad_attended, low_terms = lax.optimization_barrier((grad_attended, low_terms))
    came_low = scatter_first(low_terms)
    grad_high = attend_back(
        places, seg_keys, seg_queries, qkv, grad_attended, logsum, few, pairs - few
    )
    came_gu, grad_high, grad_low, line_gd = lax.optimization_barrier(
        (came_gu, grad_high, grad_low, line_gd)
    )
    if plane_split():
        line_gu = scatter_third(up_terms, came_gu).astype(BF16)
    else:
        line_gu = up_terms
    high_terms = dot_outer(normed1, grad_high).astype(BF16).reshape(chips, 2 * own_rows, -1)
    high_terms = [high_terms]
    if plane_split():
        down_terms = line_gd.reshape(4, -1, own_rows, width)
        down_terms = jnp.concatenate([down_terms[..., :half], down_terms[..., half:]], axis=2)
        down_terms = down_terms.transpose(1, 0, 2, 3).reshape(chips, 2 * own_rows, half)
        high_terms.append(down_terms)
    high_terms = jnp.concatenate(high_terms, axis=2)
    came_high = scatter_first(high_terms)
    near_low, high_terms, active = lax.optimization_barrier((came_low[:2], high_terms, active))
    came_low = list(near_low) + came_low[2:]
    mixed = add_cores(dot_plain, active, w_down) + b_down
    outputs = (resid + mixed).astype(BF16).reshape(-1, rows, width)

    low_width, high_width = few * PAIR, (pairs - few) * PAIR
    w_low = jnp.concatenate(
        [w_qkv[:, part * half : part * half + low_width] for part in range(3)], axis=1
    )
    w_high = jnp.concatenate(
        [w_qkv[:, part * half + low_width : (part + 1) * half] for part in range(3)], axis=1
    )
    count = grad_low.shape[0] // 2
    other = dot_back(grad_low[count:], w_low) + dot_back(grad_high[count:], w_high)
    other = swap_core(other.astype(BF16)).astype(F32)
    grad_normed1 = dot_back(grad_low[:count], w_low) + dot_back(grad_high[:count], w_high) + other
    own_x32 = own_x.astype(F32)
    _, norm1_pull = jax.vjp(norm_forward, own_x32, gain1, shift1)
    grad_part1, grad_gain1, grad_shift1 = norm1_pull(grad_normed1)
    grad_x = (grad_resid + grad_part1).reshape(-1, rows, width)

    def place_heads(sums):
        zeros = jnp.zeros((width,), F32)
        return lax.dynamic_update_slice_in_dim(zeros, sums, core * half, 0)

    low_sums = jnp.sum(grad_low.astype(F32), axis=0)
    high_sums = jnp.sum(grad_high.astype(F32), axis=0)

    def head_sums(part):
        low = low_sums[part * low_width : (part + 1) * low_width]
        high = high_sums[part * high_width : (part + 1) * high_width]
        return place_heads(jnp.concatenate([low, high]))

    small_sums = [
        grad_gain1,
        grad_shift1,
        head_sums(0),
        head_sums(2),
        jnp.sum(grad_branch_own.astype(F32), axis=0),
        grad_gain2,
        grad_shift2,
        jnp.sum(own_g32, axis=0),
    ]
    up_sums = jnp.sum(grad_pre.astype(F32), axis=0)
    small_terms = jnp.concatenate(
        [vector.reshape(chips, 2 * own_rows) for vector in small_sums]
        + [up_sums.reshape(chips, own_units)],
        axis=1,
    )
    small_width = small_terms.shape[1]
    small_terms = jnp.pad(small_terms, ((0, 0), (0, 2 * own_rows * LANES - small_width)))
    small_terms = small_terms.reshape(chips, 2 * own_rows, LANES)

    low_got = []
    if plane_split():
        line_low = scatter_third(low_terms, came_low).astype(BF16)
        low_got = line_terms(line_low)
        up_sum = lax.psum_scatter(line_gu, "z", scatter_dimension=0).astype(F32)
    came_high, low_got, grad_x = lax.optimization_barrier((came_high, low_got, grad_x))

    count = lax.axis_size("x")
    if count == 2:
        here = lax.axis_index("x")
        other = lax.ppermute(take(grad_x, 1 - here).astype(BF16), "x", SWAP).astype(F32)
        input_grad = in_order(here, take(grad_x, here), other, 0)
    else:
        input_grad = over_x(grad_x)
    if plane_split():
        low_sum = add_terms(low_got)
        line_high = scatter_third(high_terms, came_high)
        down_grad = line_high[..., 3 * high_width :]
        down_grad = jnp.concatenate([down_grad[:, :own_rows], down_grad[:, own_rows:]], axis=2)
        down_grad = down_grad.reshape(own_units, width)
        line_high = line_high[..., : 3 * high_width]
        line_high = jnp.concatenate([line_high, scatter_small(small_terms)], axis=2).astype(BF16)
        outputs = over_x(after(outputs, came_high))
        high_got = line_terms(line_high)
        high_got, input_grad, outputs = lax.optimization_barrier((high_got, input_grad, outputs))
        high_sum = add_terms(high_got)
    else:
        down_grad = lax.psum_scatter(line_gd, CHIPS, scatter_dimension=0).astype(F32)
        low_sum = scatter_end(low_terms, ())
        up_sum = scatter_end(up_terms, ())
        outputs = over_x(outputs)
        high_sum = scatter_end(jnp.concatenate([high_terms.astype(F32), small_terms], axis=2), ())
    out_sum = low_sum[:, 3 * low_width :]
    qkv_sum = jnp.concatenate(
        [
            piece
            for part in range(3)
            for piece in (
                low_sum[:, part * low_width : (part + 1) * low_width],
                high_sum[:, part * high_width : (part + 1) * high_width],
            )
        ],
        axis=1,
    )
    sums = high_sum[:, 3 * high_width :].reshape(-1)
    up_sum = up_sum.reshape(2, own_rows, mine)
    out_grad = jnp.concatenate([out_sum[:own_rows], out_sum[own_rows:]], axis=1)
    up_other = swap_core(take(up_sum, 1 - core))
    up_grad = in_order(
        core,
        take(up_sum, core).reshape(own_rows, chips, own_units),
        up_other.reshape(own_rows, chips, own_units),
        2,
    )
    up_grad = up_grad.reshape(own_rows, 2 * mine)
    weight_sum = qkv_sum.reshape(2, own_rows, 3 * half)
    qkv_other = swap_core(take(weight_sum, 1 - core))
    qkv_grad = in_order(
        core,
        take(weight_sum, core).reshape(own_rows, 3, half),
        qkv_other.reshape(own_rows, 3, half),
        2,
    )
    qkv_grad = qkv_grad.reshape(own_rows, 6 * half)
    shared = sums[: 16 * own_rows].reshape(8, 2, own_rows)
    shared = take(shared, core, 1) + swap_core(take(shared, 1 - core, 1))
    up_bias_grad = sums[16 * own_rows : 16 * own_rows + own_units]

    return (
        outputs,
        input_grad,
        shared[0],
        shared[1],
        qkv_grad,
        shared[2:4],
        out_grad,
        shared[4],
        shared[5],
        shared[6],
        up_grad,
        up_bias_grad,
        down_grad,
        shared[7],
    )


def solution(mesh):
    groups, members = mesh.devices.shape
    split = Mesh(mesh.devices.reshape(groups // 2, 2, members // 2, 2), ("z", "y", "x", "c"))
    every = ("z", "y", "x", "c")
    tokens = P(("z", "y"), ("x", "c"), None)
    vector = P(every)
    matrix = P(every, None)
    return jax.shard_map(
        per_device,
        mesh=split,
        in_specs=(
            tokens,
            P(("z", "y"), ("x", "c")),
            tokens,
            vector,
            vector,
            matrix,
            P(None, every),
            matrix,
            vector,
            vector,
            vector,
            matrix,
            vector,
            matrix,
            vector,
        ),
        out_specs=(
            tokens,
            tokens,
            vector,
            vector,
            matrix,
            P(None, every),
            matrix,
            vector,
            vector,
            vector,
            matrix,
            vector,
            matrix,
            vector,
        ),
        check_vma=False,
    )
```

```python
import functools

import jax
import jax.numpy as jnp
from jax import lax
from jax.experimental import pallas as pl
from jax.experimental.pallas import tpu as pltpu
from jax.sharding import Mesh
from jax.sharding import PartitionSpec as P

HEAD_DIM = 64
PAIR = 2 * HEAD_DIM
LANES = 128
BLOCK = 256
SWAP = [(0, 1), (1, 0)]
CHIPS = ("z", "y", "x")
BF16 = jnp.bfloat16
F32 = jnp.float32


def norm_forward(values, gain, shift):
    average = jnp.mean(values, axis=-1, keepdims=True)
    centred = values - average
    spread = jnp.mean(centred * centred, axis=-1, keepdims=True)
    return centred * lax.rsqrt(spread + 1e-05) * gain + shift


def gelu_tanh(values):
    return jax.nn.gelu(values, approximate=True)


def dot_plain(left, right):
    return jnp.dot(left, right, preferred_element_type=F32)


def dot_outer(left, right):
    return lax.dot_general(left, right, (((0,), (0,)), ((), ())), preferred_element_type=F32)


def dot_back(left, weight):
    return lax.dot_general(left, weight, (((1,), (1,)), ((), ())), preferred_element_type=F32)


def fill_bias(seg_keys, seg_queries, bias):
    total = bias.shape[0]
    for start in range(0, total, BLOCK):
        stop = start + BLOCK
        places_k = lax.broadcasted_iota(jnp.int32, (stop, BLOCK), 0)
        places_q = lax.broadcasted_iota(jnp.int32, (stop, BLOCK), 1) + start
        kept = (seg_keys[:stop, :] == seg_queries[:, start:stop]) & (places_k <= places_q)
        bias[:stop, start:stop] = jnp.where(kept, 0.0, -1000000000.0)


def piece_rows(places, first, piece):
    return pl.ds(pl.multiple_of(places[first // piece], piece), piece)


def load_rows(places, source, first, count, columns):
    piece = source.shape[0] // places.shape[0]
    return jnp.concatenate(
        [
            source[piece_rows(places, start, piece), columns]
            for start in range(first, first + count, piece)
        ],
        axis=0,
    )


def store_rows(places, target, first, count, columns, rows):
    piece = target.shape[0] // places.shape[0]
    for start in range(0, count, piece):
        target[piece_rows(places, first + start, piece), columns] = rows[start : start + piece]


def head_masks():
    lanes = lax.broadcasted_iota(jnp.int32, (1, PAIR), 1)
    return [(lanes // HEAD_DIM == head).astype(F32).astype(BF16) for head in range(2)]


def turned(values):
    return values.astype(F32).T.astype(BF16)


def forward_kernel(places, seg_keys, seg_queries, qkv, out, logsum, bias):
    step = pl.program_id(0)
    total = out.shape[0]
    width = out.shape[1]

    @pl.when(step == 0)
    def _():
        fill_bias(seg_keys, seg_queries, bias)

    column = pl.multiple_of(step * PAIR, PAIR)
    here = pl.ds(column, PAIR)
    keys = load_rows(places, qkv, 0, total, pl.ds(width + column, PAIR))
    values_t = turned(load_rows(places, qkv, 0, total, pl.ds(2 * width + column, PAIR)))
    masks = head_masks()
    for start in range(0, total, BLOCK):
        stop = start + BLOCK
        queries = load_rows(places, qkv, start, BLOCK, here)
        queries = queries * jnp.asarray(HEAD_DIM ** (-0.5), BF16)
        parts = []
        for head in range(2):
            scores = dot_back(keys[:stop], queries * masks[head]) + bias[:stop, start:stop]
            highest = jnp.max(scores, axis=0, keepdims=True)
            expon = jnp.exp(scores - highest)
            totals = jnp.sum(expon, axis=0, keepdims=True)
            first = head * HEAD_DIM
            part = dot_plain(values_t[first : first + HEAD_DIM, :stop], expon.astype(BF16))
            parts.append(part / totals)
            logsum[0, head : head + 1, start:stop] = highest + jnp.log(totals)
        rows = jnp.concatenate(parts, axis=0).T.astype(BF16)
        store_rows(places, out, start, BLOCK, here, rows)


def backward_kernel(
    first_pair, places, seg_keys, seg_queries, qkv, grad, logsum, grad_qkv, bias, sum_k, sum_v
):
    step = pl.program_id(0)
    total, width = grad.shape

    @pl.when(step == 0)
    def _():
        fill_bias(seg_keys, seg_queries, bias)

    column = pl.multiple_of((first_pair + step) * PAIR, PAIR)
    here = pl.ds(column, PAIR)
    here_k = pl.ds(width + column, PAIR)
    here_v = pl.ds(2 * width + column, PAIR)
    part_width = grad_qkv.shape[1] // 3
    part_column = pl.multiple_of(step * PAIR, PAIR)
    put_q = pl.ds(part_column, PAIR)
    put_k = pl.ds(part_width + part_column, PAIR)
    put_v = pl.ds(2 * part_width + part_column, PAIR)
    keys = load_rows(places, qkv, 0, total, here_k)
    values = load_rows(places, qkv, 0, total, here_v)
    keys_t = turned(keys)
    masks = head_masks()
    sum_k[...] = jnp.zeros_like(sum_k)
    sum_v[...] = jnp.zeros_like(sum_v)
    for start in range(0, total, BLOCK):
        stop = start + BLOCK
        queries = load_rows(places, qkv, start, BLOCK, here)
        queries = queries * jnp.asarray(HEAD_DIM ** (-0.5), BF16)
        grads = load_rows(places, grad, start, BLOCK, here)
        parts = []
        for head in range(2):
            query = queries * masks[head]
            grad_head = grads * masks[head]
            scores = dot_back(keys[:stop], query) + bias[:stop, start:stop]
            weights = jnp.exp(scores - logsum[0, head : head + 1, start:stop])
            grad_weights = dot_back(values[:stop], grad_head)
            inner = jnp.sum(weights * grad_weights, axis=0, keepdims=True)
            grad_scores = (weights * (grad_weights - inner)).astype(BF16)
            sum_v[:stop, :] += dot_plain(weights.astype(BF16), grad_head)
            sum_k[:stop, :] += dot_plain(grad_scores, query)
            first = head * HEAD_DIM
            parts.append(dot_plain(keys_t[first : first + HEAD_DIM, :stop], grad_scores))
        grad_queries = jnp.concatenate(parts, axis=0).T * HEAD_DIM ** (-0.5)
        store_rows(places, grad_qkv, start, BLOCK, put_q, grad_queries.astype(BF16))
    store_rows(places, grad_qkv, 0, total, put_k, sum_k[...].astype(BF16))
    store_rows(places, grad_qkv, 0, total, put_v, sum_v[...].astype(BF16))


def whole_block(shape):
    return pl.BlockSpec(shape, lambda step: (0,) * len(shape))


def attend(places, seg_keys, seg_queries, qkv):
    total, width3 = qkv.shape
    width = width3 // 3
    pairs = width // PAIR
    return pl.pallas_call(
        forward_kernel,
        grid=(pairs,),
        in_specs=[
            pl.BlockSpec(memory_space=pltpu.SMEM),
            whole_block((total, 1)),
            whole_block((1, total)),
            whole_block((total, width3)),
        ],
        out_specs=[
            whole_block((total, width)),
            pl.BlockSpec((1, 2, total), lambda step: (step, 0, 0)),
        ],
        out_shape=[
            jax.ShapeDtypeStruct((total, width), BF16),
            jax.ShapeDtypeStruct((pairs, 2, total), F32),
        ],
        scratch_shapes=[pltpu.VMEM((total, total), F32)],
        compiler_params=pltpu.CompilerParams(vmem_limit_bytes=48 * 1024 * 1024),
        cost_estimate=pl.CostEstimate(
            flops=40 * total * total * width, bytes_accessed=total * width, transcendentals=0
        ),
        name="attention_forward",
    )(places, seg_keys, seg_queries, qkv)


def attend_back(places, seg_keys, seg_queries, qkv, grad, logsum, first, pairs):
    total, width = grad.shape
    return pl.pallas_call(
        functools.partial(backward_kernel, first),
        grid=(pairs,),
        in_specs=[
            pl.BlockSpec(memory_space=pltpu.SMEM),
            whole_block((total, 1)),
            whole_block((1, total)),
            whole_block((total, 3 * width)),
            whole_block((total, width)),
            pl.BlockSpec((1, 2, total), lambda step: (first + step, 0, 0)),
        ],
        out_specs=whole_block((total, 3 * pairs * PAIR)),
        out_shape=jax.ShapeDtypeStruct((total, 3 * pairs * PAIR), BF16),
        scratch_shapes=[
            pltpu.VMEM((total, total), F32),
            pltpu.VMEM((total, PAIR), F32),
            pltpu.VMEM((total, PAIR), F32),
        ],
        compiler_params=pltpu.CompilerParams(vmem_limit_bytes=48 * 1024 * 1024),
        cost_estimate=pl.CostEstimate(
            flops=total * total, bytes_accessed=total * width, transcendentals=0
        ),
        name="attention_backward",
    )(places, seg_keys, seg_queries, qkv, grad, logsum)


def pack_kernel(core, qkv, up, segments, *refs):
    vectors, (send_qkv, keep_qkv, send_up, keep_up) = refs[:-4], refs[-4:]
    rows, width3 = qkv.shape
    half = width3 // 6
    blocks = up.shape[1] // (2 * LANES)
    for place, to_qkv, to_up in ((1 - core[0], send_qkv, send_up), (core[0], keep_qkv, keep_up)):
        for part in range(3):
            start = pl.multiple_of(2 * part * half + place * half, half)
            to_qkv[:, part * half : (part + 1) * half] = qkv[:, pl.ds(start, half)]
        to_qkv[:, 3 * half :] = jnp.zeros((rows, LANES), BF16)
        row = 0
        for vector in vectors:
            count, size = vector.shape
            to_qkv[row : row + count, 3 * half : 3 * half + size] = vector[...]
            row += count
        for sequence in range(segments.shape[0]):
            for start in range(0, segments.shape[1], LANES):
                numbers = segments[sequence : sequence + 1, start : start + LANES]
                to_qkv[row : row + 1, 3 * half :] = numbers.astype(F32).astype(BF16)
                row += 1
        for block in range(blocks):
            start = pl.multiple_of((2 * block + place) * LANES, LANES)
            to_up[:, block * LANES : (block + 1) * LANES] = up[:, pl.ds(start, LANES)]


def pack(core, qkv, up, segments, vectors):
    rows = qkv.shape[0]
    shape_qkv = jax.ShapeDtypeStruct((rows, qkv.shape[1] // 2 + LANES), BF16)
    shape_up = jax.ShapeDtypeStruct((rows, up.shape[1] // 2), BF16)
    vmem = pl.BlockSpec(memory_space=pltpu.VMEM)
    vectors = [vector if vector.ndim == 2 else vector[None] for vector in vectors]
    return pl.pallas_call(
        pack_kernel,
        in_specs=[pl.BlockSpec(memory_space=pltpu.SMEM)] + [vmem] * (3 + len(vectors)),
        out_specs=[vmem] * 4,
        out_shape=[shape_qkv, shape_qkv, shape_up, shape_up],
        name="pack_weights",
    )(core.reshape(1), qkv, up, segments, *vectors)


def beside_kernel(splits, place, line, from_x, from_y, *outs):
    rows = line.shape[1]
    y, x = place[0], place[1]
    for part, py, px in ((line, y, x), (from_x, y, 1 - x), (from_y, 1 - y, x)):
        target = pl.ds(pl.multiple_of((2 * py + px) * rows, rows), rows)
        for out, (start, stop) in zip(outs, splits):
            out[target, :] = part[0, :, start:stop]


def corner_kernel(splits, place, low, high, *refs):
    outs = refs[len(refs) // 2 :]
    half = low.shape[1]
    for out, (start, stop) in zip(outs, splits):
        out[:, 0, :half, :] = low[:, :, start:stop]
        out[:, 0, half:, :] = high[:, :, start:stop]


def put_beside(place, line, from_x, from_y, splits):
    lines, rows, columns = line.shape
    part = pl.BlockSpec((1, rows, columns), lambda step, place: (step, 0, 0))
    return pl.pallas_call(
        functools.partial(beside_kernel, splits),
        grid_spec=pltpu.PrefetchScalarGridSpec(
            num_scalar_prefetch=1,
            grid=(lines,),
            in_specs=[part] * 3,
            out_specs=[
                pl.BlockSpec((4 * rows, stop - start), lambda step, place: (step, 0))
                for start, stop in splits
            ],
        ),
        out_shape=[
            jax.ShapeDtypeStruct((lines * 4 * rows, stop - start), line.dtype)
            for start, stop in splits
        ],
        cost_estimate=pl.CostEstimate(
            flops=6144 * line.size, bytes_accessed=8 * line.size, transcendentals=0
        ),
        name="put_beside",
    )(place, line, from_x, from_y)


def put_corner(place, low, high, wholes, splits):
    lines, half, columns = low.shape

    def there(step, place):
        return (0, 2 * (1 - place[0]) + 1 - place[1], 0, 0)

    part = pl.BlockSpec(low.shape, lambda step, place: (0, 0, 0))
    wholes = [whole.reshape(lines, 4, 2 * half, -1) for whole in wholes]
    return pl.pallas_call(
        functools.partial(corner_kernel, splits),
        grid_spec=pltpu.PrefetchScalarGridSpec(
            num_scalar_prefetch=1,
            grid=(1,),
            in_specs=[part] * 2 + [pl.BlockSpec(memory_space=pl.ANY)] * len(wholes),
            out_specs=[
                pl.BlockSpec((lines, 1, 2 * half, stop - start), there) for start, stop in splits
            ],
        ),
        out_shape=[jax.ShapeDtypeStruct(whole.shape, whole.dtype) for whole in wholes],
        input_output_aliases={3 + place: place for place in range(len(wholes))},
        name="put_corner",
    )(place, low, high, *wholes)


def join_kernel(first, second, out):
    count = first.shape[0]
    out[:count] = first[...]
    out[count:] = second[...]


def join(first, second):
    count, columns = first.shape
    half = pl.BlockSpec((count, columns // 2), lambda step: (0, step))
    return pl.pallas_call(
        join_kernel,
        grid=(2,),
        in_specs=[half, half],
        out_specs=pl.BlockSpec((2 * count, columns // 2), lambda step: (0, step)),
        out_shape=jax.ShapeDtypeStruct((2 * count, columns), first.dtype),
        name="join",
    )(first, second)


def swap_core(array):
    return lax.ppermute(array, "c", SWAP)


def take(array, place, axis=0):
    return lax.dynamic_index_in_dim(array, place, axis, keepdims=False)


def in_order(place, own, other, axis):
    first = jnp.stack([own, other], axis=axis)
    second = jnp.stack([other, own], axis=axis)
    return jnp.where(place == 0, first, second)


def over_x(array):
    count = lax.axis_size("x")
    if count != 2:
        return lax.all_to_all(array, "x", 0, 0)
    here = lax.axis_index("x")
    other = lax.ppermute(take(array, 1 - here), "x", SWAP)
    return in_order(here, take(array, here), other, 0)


def plane_split():
    return tuple(lax.axis_size(name) for name in CHIPS) == (4, 2, 2)


def after(array, *others):
    return lax.optimization_barrier((array, others))[0]


def turn_z(step):
    size = lax.axis_size("z")
    return [(place, (place + step) % size) for place in range(size)]


def gather_line(chunk):
    if not plane_split():
        return chunk
    size, z = lax.axis_size("z"), lax.axis_index("z")
    full = jnp.broadcast_to(chunk, (size,) + chunk.shape)
    for step in range(1, size):
        part = lax.ppermute(chunk, "z", turn_z(step))
        full = lax.dynamic_update_index_in_dim(full, part, (z + size - step) % size, 0)
    return full


def gather_first(line):
    if not plane_split():
        return ()
    return lax.ppermute(line, "x", SWAP), lax.ppermute(line, "y", SWAP)


def gather_second(line, came):
    if not plane_split():
        return ()
    half = line.shape[1] // 2
    from_x, from_y = came
    corner_low = lax.ppermute(from_x[:, :half], "y", SWAP)
    corner_high = lax.ppermute(from_y[:, half:], "x", SWAP)
    return corner_low, corner_high


def gather_whole(line, came, corner, *splits):
    if not plane_split():
        full = lax.all_gather(line, CHIPS).reshape(-1, line.shape[-1])
        return [full[:, start:stop] for start, stop in splits]
    place = jnp.stack([lax.axis_index("y"), lax.axis_index("x")]).astype(jnp.int32)
    wholes = put_beside(place, line, *came, splits)
    wholes = put_corner(place, *corner, wholes, splits)
    return [whole.reshape(-1, whole.shape[-1]) for whole in wholes]


def add_low(*parts):
    return functools.reduce(jnp.add, [part.astype(F32) for part in parts]).astype(BF16)


def plane_turns():
    for step_y, step_x in ((0, 1), (1, 0), (1, 1)):
        turn = [(place, place ^ (2 * step_y + step_x)) for place in range(4)]
        yield step_y, step_x, turn


def plane_part(chunks, step_y, step_x):
    y, x = lax.axis_index("y"), lax.axis_index("x")
    split = chunks.reshape((-1, 4) + chunks.shape[1:])
    return take(split, 2 * (y ^ step_y) + (x ^ step_x), 1)


def scatter_first(chunks):
    if not plane_split():
        return []
    return [
        lax.ppermute(plane_part(chunks, step_y, step_x), ("y", "x"), turn)
        for step_y, step_x, turn in plane_turns()
    ]


def scatter_third(chunks, came):
    return add_terms([plane_part(chunks, 0, 0)] + list(came))


def line_terms(line):
    size, z = lax.axis_size("z"), lax.axis_index("z")
    return [take(line, z)] + [
        lax.ppermute(take(line, (z + step) % size), "z", turn_z(step)) for step in range(1, size)
    ]


def add_terms(terms):
    return functools.reduce(jnp.add, [term.astype(F32) for term in terms])


def scatter_line(line):
    return add_terms(line_terms(line))


def scatter_end(chunks, came, *others):
    if not plane_split():
        return lax.psum_scatter(chunks, CHIPS, scatter_dimension=0).astype(F32)
    return scatter_line(scatter_third(chunks, came).astype(BF16), *others)


def scatter_small(terms):
    return scatter_third(terms, scatter_first(terms))


def per_device(
    inputs,
    segments,
    cotangent,
    ln1_gain,
    ln1_shift,
    qkv_weight,
    qv_bias,
    out_weight,
    out_bias,
    ln2_gain,
    ln2_shift,
    up_weight,
    up_bias,
    down_weight,
    down_bias,
):
    _, rows, width = inputs.shape
    own_rows = out_weight.shape[0]
    own_units = down_weight.shape[0]
    chips = width // (2 * own_rows)
    core = lax.axis_index("c")
    half = width // 2
    mine = 2 * chips * own_units // 2

    seg_rows = segments.size // LANES
    in_rows = own_units % LANES == 0 and rows % LANES == 0 and own_rows >= 9 + seg_rows
    if in_rows:
        vectors = (ln1_gain, ln1_shift, qv_bias, out_bias, ln2_gain, ln2_shift, down_bias, up_bias)
        packed = pack(core, qkv_weight, up_weight, segments, vectors)
    else:
        small = jnp.concatenate(
            [ln1_gain, ln1_shift, qv_bias[0], qv_bias[1], out_bias, ln2_gain, ln2_shift, down_bias]
            + [up_bias]
        )
        small_count = small.shape[0]
        small = jnp.pad(small, (0, own_rows * LANES - small_count)).reshape(own_rows, LANES)

        def head_columns(place):
            columns = [
                lax.dynamic_slice_in_dim(qkv_weight, part * width + place * half, half, 1)
                for part in range(3)
            ]
            return jnp.concatenate(columns + [small], axis=1)

        up_split = up_weight.reshape(own_rows, chips, 2, own_units)
        packed = (
            head_columns(1 - core),
            head_columns(core),
            take(up_split, 1 - core, 2).reshape(own_rows, mine),
            take(up_split, core, 2).reshape(own_rows, mine),
        )
    send_qkv, keep_qkv, send_up, keep_up = packed
    chunk_qkv = in_order(core, keep_qkv, swap_core(send_qkv), 0).reshape(2 * own_rows, -1)
    send_up = after(send_up, chunk_qkv)
    chunk_up = in_order(core, keep_up, swap_core(send_up), 0).reshape(2 * own_rows, -1)
    chunk_out = jnp.concatenate([out_weight[:, :half], out_weight[:, half:]], axis=0)
    chunk_up = jnp.concatenate([chunk_up, chunk_out], axis=1)

    def both_cores(own):
        return join(own, swap_core(own))

    def joined(array):
        return array.reshape((-1,) + array.shape[2:])

    line_qkv = gather_line(chunk_qkv)
    if lax.axis_size("x") == 2:
        here = lax.axis_index("x")
        other = lax.ppermute(take(inputs, 1 - here), "x", SWAP)
        own_x = in_order(here, take(inputs, here), other, 0)
    else:
        own_x = over_x(inputs)
    own_x = joined(own_x)
    total = 2 * own_x.shape[0]
    pieces = jnp.arange(total // rows, dtype=jnp.int32)
    places = jnp.where(pieces % 2 == core, 0, own_x.shape[0]) + pieces // 2 * rows

    line_up = lax.all_gather(chunk_up, "z") if plane_split() else chunk_up
    line_qkv = after(line_qkv, own_x, chunk_up)
    came_qkv = gather_first(line_qkv)
    full_x = both_cores(own_x)
    line_down, came_down = down_weight[None], ()
    if plane_split():
        line_down = after(line_down, came_qkv)
        came_down = gather_first(line_down)
    full_x = full_x.astype(F32)
    corner_qkv = gather_second(line_qkv, came_qkv)
    plane_down = down_weight
    if plane_split():
        corner_down = gather_second(line_down, came_down)
        plane_down = gather_whole(line_down, came_down, corner_down, (0, width))[0]
    corner_qkv, plane_down = lax.optimization_barrier((corner_qkv, plane_down))
    w_qkv, smalls = gather_whole(
        line_qkv, came_qkv, corner_qkv, (0, 3 * half), (3 * half, 3 * half + LANES)
    )
    smalls = smalls.reshape(2 * chips, own_rows, LANES)
    if in_rows:
        vectors = [smalls[:, place, :own_rows] for place in range(8)]
        small_up = smalls[:, 8, :own_units]
    else:
        smalls = smalls.reshape(2 * chips, -1)
        vectors = [smalls[:, place * own_rows : (place + 1) * own_rows] for place in range(8)]
        small_up = smalls[:, 8 * own_rows : 8 * own_rows + own_units]
    vectors = [vector.reshape(width).astype(F32) for vector in vectors]
    if in_rows:
        seg_all = smalls[:, 9 : 9 + seg_rows].reshape(-1, lax.axis_size("x"), 2, segments.size)
        seg_all = take(seg_all, lax.axis_index("z") * lax.axis_size("y") + lax.axis_index("y"))
        seg_all = seg_all.reshape((-1, 2) + segments.shape)
        seg_all = take(seg_all, lax.axis_index("x"), 2).reshape(-1).astype(jnp.int32)
    else:
        own_seg = over_x(segments)
        seg_all = in_order(core, own_seg, swap_core(own_seg), 1).reshape(-1)
    seg_keys = seg_all[:, None]
    seg_queries = seg_all[None, :]
    gain1, shift1, b_q, b_v, b_out, gain2, shift2, b_down = vectors
    b_up = take(small_up.reshape(chips, 2, own_units), core, 1)
    b_up = b_up.reshape(mine).astype(F32)

    normed1 = norm_forward(full_x, gain1, shift1).astype(BF16)
    normed1, line_up = lax.optimization_barrier((normed1, line_up))
    b_qkv = jnp.concatenate(
        [
            lax.dynamic_slice_in_dim(b_q, core * half, half),
            jnp.zeros((half,), F32),
            lax.dynamic_slice_in_dim(b_v, core * half, half),
        ]
    )
    qkv = (dot_plain(normed1, w_qkv) + b_qkv).astype(BF16)
    w_down = lax.all_gather(plane_down, "z" if plane_split() else CHIPS).reshape(mine, width)
    line_up = after(line_up, corner_qkv)
    came_up = gather_first(line_up)
    attended, logsum = attend(places, seg_keys, seg_queries, qkv)
    attended = after(attended, came_up)
    came_up = after(came_up, attended)
    corner_up = gather_second(line_up, came_up)
    w_up, all_out = gather_whole(
        line_up, came_up, corner_up, (0, mine), (mine, mine + half)
    )
    all_out = all_out.reshape(chips, 2 * own_rows, half)
    all_out = jnp.concatenate([all_out[:, :own_rows], all_out[:, own_rows:]], axis=2)
    out_keep = lax.dynamic_slice_in_dim(all_out, core * (chips // 2), chips // 2)
    out_send = lax.dynamic_slice_in_dim(all_out, (1 - core) * (chips // 2), chips // 2)
    w_out = in_order(core, out_keep, swap_core(out_send), 1).reshape(half, width)

    def add_cores(dot, left, weight):
        count = left.shape[0] // 2
        other = swap_core(dot(left[count:], weight).astype(BF16))
        return dot(left[:count], weight) + other.astype(F32)

    own_g = joined(over_x(after(cotangent, came_up)))
    attended, own_g = lax.optimization_barrier((attended, own_g))
    resid = own_x.astype(F32) + add_cores(dot_plain, attended, w_out) + b_out
    normed2_own = norm_forward(resid, gain2, shift2).astype(BF16)
    normed2 = both_cores(normed2_own)
    normed2, w_down = lax.optimization_barrier((normed2, w_down))
    full_g = both_cores(own_g)
    pre = dot_plain(normed2, w_up) + b_up
    active, gelu_pull = jax.vjp(gelu_tanh, pre)
    active = active.astype(BF16)
    slope = gelu_pull(jnp.ones_like(pre))[0].astype(BF16)
    active, slope = lax.optimization_barrier((active, slope))
    grad_down = dot_outer(active, full_g).astype(BF16).reshape(chips, own_units, width)
    full_g, grad_down = lax.optimization_barrier((full_g, grad_down))
    if plane_split():
        line_gd = lax.psum_scatter(
            grad_down.reshape(-1, 4, own_units, width), "z", scatter_dimension=0
        )
    else:
        line_gd = grad_down
    grad_active = dot_back(full_g, w_down)
    grad_pre = (grad_active * slope.astype(F32)).astype(BF16)
    up_terms = dot_outer(normed2, grad_pre).astype(BF16).reshape(chips, 2 * own_rows, mine)
    grad_pre, up_terms = lax.optimization_barrier((grad_pre, up_terms))
    came_gu = scatter_first(up_terms)
    grad_normed2 = add_cores(dot_back, grad_pre, w_up)
    own_g32 = own_g.astype(F32)
    _, norm2_pull = jax.vjp(norm_forward, resid, gain2, shift2)
    grad_part, grad_gain2, grad_shift2 = norm2_pull(grad_normed2)
    grad_resid = own_g32 + grad_part

    grad_branch_own = grad_resid.astype(BF16)
    grad_branch = both_cores(grad_branch_own)
    grad_attended = dot_back(grad_branch, w_out).astype(BF16)
    grad_out = dot_outer(attended, grad_branch).astype(BF16)
    grad_out = grad_out.reshape(chips // 2, 2, own_rows, width)
    out_other = swap_core(take(grad_out, 1 - core, 1))
    out_terms = in_order(core, take(grad_out, core, 1), out_other, 0)
    out_terms = out_terms.reshape(chips, own_rows, width)
    out_terms = jnp.concatenate([out_terms[..., :half], out_terms[..., half:]], axis=1)
    pairs = half // PAIR
    few = pairs // 2
    grad_low = attend_back(places, seg_keys, seg_queries, qkv, grad_attended, logsum, 0, few)
    low_terms = dot_outer(normed1, grad_low).astype(BF16).reshape(chips, 2 * own_rows, -1)
    low_terms = jnp.concatenate([low_terms, out_terms], axis=2)
    grad_attended, low_terms = lax.optimization_barrier((grad_attended, low_terms))
    came_low = scatter_first(low_terms)
    grad_high = attend_back(
        places, seg_keys, seg_queries, qkv, grad_attended, logsum, few, pairs - few
    )
    came_gu, grad_high, grad_low, line_gd = lax.optimization_barrier(
        (came_gu, grad_high, grad_low, line_gd)
    )
    if plane_split():
        line_gu = scatter_third(up_terms, came_gu).astype(BF16)
    else:
        line_gu = up_terms
    high_terms = dot_outer(normed1, grad_high).astype(BF16).reshape(chips, 2 * own_rows, -1)
    high_terms = [high_terms]
    if plane_split():
        down_terms = line_gd.reshape(4, -1, own_rows, width)
        down_terms = jnp.concatenate([down_terms[..., :half], down_terms[..., half:]], axis=2)
        down_terms = down_terms.transpose(1, 0, 2, 3).reshape(chips, 2 * own_rows, half)
        high_terms.append(down_terms)
    high_terms = jnp.concatenate(high_terms, axis=2)
    came_high = scatter_first(high_terms)
    near_low, high_terms, active = lax.optimization_barrier((came_low[:2], high_terms, active))
    came_low = list(near_low) + came_low[2:]
    mixed = add_cores(dot_plain, active, w_down) + b_down
    outputs = (resid + mixed).astype(BF16).reshape(-1, rows, width)

    low_width, high_width = few * PAIR, (pairs - few) * PAIR
    w_low = jnp.concatenate(
        [w_qkv[:, part * half : part * half + low_width] for part in range(3)], axis=1
    )
    w_high = jnp.concatenate(
        [w_qkv[:, part * half + low_width : (part + 1) * half] for part in range(3)], axis=1
    )
    count = grad_low.shape[0] // 2
    other = dot_back(grad_low[count:], w_low) + dot_back(grad_high[count:], w_high)
    other = swap_core(other.astype(BF16)).astype(F32)
    grad_normed1 = dot_back(grad_low[:count], w_low) + dot_back(grad_high[:count], w_high) + other
    own_x32 = own_x.astype(F32)
    _, norm1_pull = jax.vjp(norm_forward, own_x32, gain1, shift1)
    grad_part1, grad_gain1, grad_shift1 = norm1_pull(grad_normed1)
    grad_x = (grad_resid + grad_part1).reshape(-1, rows, width)

    def place_heads(sums):
        zeros = jnp.zeros((width,), F32)
        return lax.dynamic_update_slice_in_dim(zeros, sums, core * half, 0)

    low_sums = jnp.sum(grad_low.astype(F32), axis=0)
    high_sums = jnp.sum(grad_high.astype(F32), axis=0)

    def head_sums(part):
        low = low_sums[part * low_width : (part + 1) * low_width]
        high = high_sums[part * high_width : (part + 1) * high_width]
        return place_heads(jnp.concatenate([low, high]))

    small_sums = [
        grad_gain1,
        grad_shift1,
        head_sums(0),
        head_sums(2),
        jnp.sum(grad_branch_own.astype(F32), axis=0),
        grad_gain2,
        grad_shift2,
        jnp.sum(own_g32, axis=0),
    ]
    up_sums = jnp.sum(grad_pre.astype(F32), axis=0)
    small_terms = jnp.concatenate(
        [vector.reshape(chips, 2 * own_rows) for vector in small_sums]
        + [up_sums.reshape(chips, own_units)],
        axis=1,
    )
    small_width = small_terms.shape[1]
    small_terms = jnp.pad(small_terms, ((0, 0), (0, 2 * own_rows * LANES - small_width)))
    small_terms = small_terms.reshape(chips, 2 * own_rows, LANES)

    low_got = []
    if plane_split():
        line_low = scatter_third(low_terms, came_low).astype(BF16)
        low_got = line_terms(line_low)
        up_sum = lax.psum_scatter(line_gu, "z", scatter_dimension=0).astype(F32)
    came_high, low_got, grad_x, small_terms = lax.optimization_barrier(
        (came_high, low_got, grad_x, small_terms)
    )

    count = lax.axis_size("x")
    if count == 2:
        here = lax.axis_index("x")
        other = lax.ppermute(take(grad_x, 1 - here).astype(BF16), "x", SWAP).astype(F32)
        input_grad = in_order(here, take(grad_x, here), other, 0)
    else:
        input_grad = over_x(grad_x)
    if plane_split():
        low_sum = add_terms(low_got)
        line_high = scatter_third(high_terms, came_high)
        down_grad = line_high[..., 3 * high_width :]
        down_grad = jnp.concatenate([down_grad[:, :own_rows], down_grad[:, own_rows:]], axis=2)
        down_grad = down_grad.reshape(own_units, width)
        line_high = line_high[..., : 3 * high_width]
        line_high = jnp.concatenate([line_high, scatter_small(small_terms)], axis=2).astype(BF16)
        outputs = over_x(after(outputs, came_high))
        high_got = line_terms(line_high)
        high_got, input_grad, outputs = lax.optimization_barrier((high_got, input_grad, outputs))
        high_sum = add_terms(high_got)
    else:
        down_grad = lax.psum_scatter(line_gd, CHIPS, scatter_dimension=0).astype(F32)
        low_sum = scatter_end(low_terms, ())
        up_sum = scatter_end(up_terms, ())
        outputs = over_x(outputs)
        high_sum = scatter_end(jnp.concatenate([high_terms.astype(F32), small_terms], axis=2), ())
    out_sum = low_sum[:, 3 * low_width :]
    qkv_sum = jnp.concatenate(
        [
            piece
            for part in range(3)
            for piece in (
                low_sum[:, part * low_width : (part + 1) * low_width],
                high_sum[:, part * high_width : (part + 1) * high_width],
            )
        ],
        axis=1,
    )
    sums = high_sum[:, 3 * high_width :].reshape(-1)
    up_sum = up_sum.reshape(2, own_rows, mine)
    out_grad = jnp.concatenate([out_sum[:own_rows], out_sum[own_rows:]], axis=1)
    up_other = swap_core(take(up_sum, 1 - core))
    up_grad = in_order(
        core,
        take(up_sum, core).reshape(own_rows, chips, own_units),
        up_other.reshape(own_rows, chips, own_units),
        2,
    )
    up_grad = up_grad.reshape(own_rows, 2 * mine)
    weight_sum = qkv_sum.reshape(2, own_rows, 3 * half)
    qkv_other = swap_core(take(weight_sum, 1 - core))
    qkv_grad = in_order(
        core,
        take(weight_sum, core).reshape(own_rows, 3, half),
        qkv_other.reshape(own_rows, 3, half),
        2,
    )
    qkv_grad = qkv_grad.reshape(own_rows, 6 * half)
    shared = sums[: 16 * own_rows].reshape(8, 2, own_rows)
    shared = take(shared, core, 1) + swap_core(take(shared, 1 - core, 1))
    up_bias_grad = sums[16 * own_rows : 16 * own_rows + own_units]

    return (
        outputs,
        input_grad,
        shared[0],
        shared[1],
        qkv_grad,
        shared[2:4],
        out_grad,
        shared[4],
        shared[5],
        shared[6],
        up_grad,
        up_bias_grad,
        down_grad,
        shared[7],
    )


def solution(mesh):
    groups, members = mesh.devices.shape
    split = Mesh(mesh.devices.reshape(groups // 2, 2, members // 2, 2), ("z", "y", "x", "c"))
    every = ("z", "y", "x", "c")
    tokens = P(("z", "y"), ("x", "c"), None)
    vector = P(every)
    matrix = P(every, None)
    return jax.shard_map(
        per_device,
        mesh=split,
        in_specs=(
            tokens,
            P(("z", "y"), ("x", "c")),
            tokens,
            vector,
            vector,
            matrix,
            P(None, every),
            matrix,
            vector,
            vector,
            vector,
            matrix,
            vector,
            matrix,
            vector,
        ),
        out_specs=(
            tokens,
            tokens,
            vector,
            vector,
            matrix,
            P(None, every),
            matrix,
            vector,
            vector,
            vector,
            matrix,
            vector,
            matrix,
            vector,
        ),
        check_vma=False,
    )
```

```python
import functools

import jax
import jax.numpy as jnp
from jax import lax
from jax.experimental import pallas as pl
from jax.experimental.pallas import tpu as pltpu
from jax.sharding import Mesh
from jax.sharding import PartitionSpec as P

HEAD_DIM = 64
PAIR = 2 * HEAD_DIM
LANES = 128
BLOCK = 256
SWAP = [(0, 1), (1, 0)]
CHIPS = ("z", "y", "x")
BF16 = jnp.bfloat16
F32 = jnp.float32


def norm_forward(values, gain, shift):
    average = jnp.mean(values, axis=-1, keepdims=True)
    centred = values - average
    spread = jnp.mean(centred * centred, axis=-1, keepdims=True)
    return centred * lax.rsqrt(spread + 1e-05) * gain + shift


def gelu_tanh(values):
    return jax.nn.gelu(values, approximate=True)


def dot_plain(left, right):
    return jnp.dot(left, right, preferred_element_type=F32)


def dot_outer(left, right):
    return lax.dot_general(left, right, (((0,), (0,)), ((), ())), preferred_element_type=F32)


def dot_back(left, weight):
    return lax.dot_general(left, weight, (((1,), (1,)), ((), ())), preferred_element_type=F32)


def fill_bias(seg_keys, seg_queries, bias):
    total = bias.shape[0]
    for start in range(0, total, BLOCK):
        stop = start + BLOCK
        places_k = lax.broadcasted_iota(jnp.int32, (stop, BLOCK), 0)
        places_q = lax.broadcasted_iota(jnp.int32, (stop, BLOCK), 1) + start
        kept = (seg_keys[:stop, :] == seg_queries[:, start:stop]) & (places_k <= places_q)
        bias[:stop, start:stop] = jnp.where(kept, 0.0, -1000000000.0)


def piece_rows(places, first, piece):
    return pl.ds(pl.multiple_of(places[first // piece], piece), piece)


def load_rows(places, source, first, count, columns):
    piece = source.shape[0] // places.shape[0]
    return jnp.concatenate(
        [
            source[piece_rows(places, start, piece), columns]
            for start in range(first, first + count, piece)
        ],
        axis=0,
    )


def store_rows(places, target, first, count, columns, rows):
    piece = target.shape[0] // places.shape[0]
    for start in range(0, count, piece):
        target[piece_rows(places, first + start, piece), columns] = rows[start : start + piece]


def head_masks():
    lanes = lax.broadcasted_iota(jnp.int32, (1, PAIR), 1)
    return [(lanes // HEAD_DIM == head).astype(F32).astype(BF16) for head in range(2)]


def turned(values):
    return values.astype(F32).T.astype(BF16)


def forward_kernel(places, seg_keys, seg_queries, qkv, out, logsum, bias):
    step = pl.program_id(0)
    total = out.shape[0]
    width = out.shape[1]

    @pl.when(step == 0)
    def _():
        fill_bias(seg_keys, seg_queries, bias)

    column = pl.multiple_of(step * PAIR, PAIR)
    here = pl.ds(column, PAIR)
    keys = load_rows(places, qkv, 0, total, pl.ds(width + column, PAIR))
    values_t = turned(load_rows(places, qkv, 0, total, pl.ds(2 * width + column, PAIR)))
    masks = head_masks()
    for start in range(0, total, BLOCK):
        stop = start + BLOCK
        queries = load_rows(places, qkv, start, BLOCK, here)
        queries = queries * jnp.asarray(HEAD_DIM ** (-0.5), BF16)
        parts = []
        for head in range(2):
            scores = dot_back(keys[:stop], queries * masks[head]) + bias[:stop, start:stop]
            highest = jnp.max(scores, axis=0, keepdims=True)
            expon = jnp.exp(scores - highest)
            totals = jnp.sum(expon, axis=0, keepdims=True)
            first = head * HEAD_DIM
            part = dot_plain(values_t[first : first + HEAD_DIM, :stop], expon.astype(BF16))
            parts.append(part / totals)
            logsum[0, head : head + 1, start:stop] = highest + jnp.log(totals)
        rows = jnp.concatenate(parts, axis=0).T.astype(BF16)
        store_rows(places, out, start, BLOCK, here, rows)


def backward_kernel(
    first_pair, places, seg_keys, seg_queries, qkv, grad, logsum, grad_qkv, bias, sum_k, sum_v
):
    step = pl.program_id(0)
    total, width = grad.shape

    @pl.when(step == 0)
    def _():
        fill_bias(seg_keys, seg_queries, bias)

    column = pl.multiple_of((first_pair + step) * PAIR, PAIR)
    here = pl.ds(column, PAIR)
    here_k = pl.ds(width + column, PAIR)
    here_v = pl.ds(2 * width + column, PAIR)
    part_width = grad_qkv.shape[1] // 3
    part_column = pl.multiple_of(step * PAIR, PAIR)
    put_q = pl.ds(part_column, PAIR)
    put_k = pl.ds(part_width + part_column, PAIR)
    put_v = pl.ds(2 * part_width + part_column, PAIR)
    keys = load_rows(places, qkv, 0, total, here_k)
    values = load_rows(places, qkv, 0, total, here_v)
    keys_t = turned(keys)
    masks = head_masks()
    sum_k[...] = jnp.zeros_like(sum_k)
    sum_v[...] = jnp.zeros_like(sum_v)
    for start in range(0, total, BLOCK):
        stop = start + BLOCK
        queries = load_rows(places, qkv, start, BLOCK, here)
        queries = queries * jnp.asarray(HEAD_DIM ** (-0.5), BF16)
        grads = load_rows(places, grad, start, BLOCK, here)
        parts = []
        for head in range(2):
            query = queries * masks[head]
            grad_head = grads * masks[head]
            scores = dot_back(keys[:stop], query) + bias[:stop, start:stop]
            weights = jnp.exp(scores - logsum[0, head : head + 1, start:stop])
            grad_weights = dot_back(values[:stop], grad_head)
            inner = jnp.sum(weights * grad_weights, axis=0, keepdims=True)
            grad_scores = (weights * (grad_weights - inner)).astype(BF16)
            sum_v[:stop, :] += dot_plain(weights.astype(BF16), grad_head)
            sum_k[:stop, :] += dot_plain(grad_scores, query)
            first = head * HEAD_DIM
            parts.append(dot_plain(keys_t[first : first + HEAD_DIM, :stop], grad_scores))
        grad_queries = jnp.concatenate(parts, axis=0).T * HEAD_DIM ** (-0.5)
        store_rows(places, grad_qkv, start, BLOCK, put_q, grad_queries.astype(BF16))
    store_rows(places, grad_qkv, 0, total, put_k, sum_k[...].astype(BF16))
    store_rows(places, grad_qkv, 0, total, put_v, sum_v[...].astype(BF16))


def whole_block(shape):
    return pl.BlockSpec(shape, lambda step: (0,) * len(shape))


def attend(places, seg_keys, seg_queries, qkv):
    total, width3 = qkv.shape
    width = width3 // 3
    pairs = width // PAIR
    return pl.pallas_call(
        forward_kernel,
        grid=(pairs,),
        in_specs=[
            pl.BlockSpec(memory_space=pltpu.SMEM),
            whole_block((total, 1)),
            whole_block((1, total)),
            whole_block((total, width3)),
        ],
        out_specs=[
            whole_block((total, width)),
            pl.BlockSpec((1, 2, total), lambda step: (step, 0, 0)),
        ],
        out_shape=[
            jax.ShapeDtypeStruct((total, width), BF16),
            jax.ShapeDtypeStruct((pairs, 2, total), F32),
        ],
        scratch_shapes=[pltpu.VMEM((total, total), F32)],
        compiler_params=pltpu.CompilerParams(vmem_limit_bytes=48 * 1024 * 1024),
        cost_estimate=pl.CostEstimate(
            flops=40 * total * total * width, bytes_accessed=total * width, transcendentals=0
        ),
        name="attention_forward",
    )(places, seg_keys, seg_queries, qkv)


def attend_back(places, seg_keys, seg_queries, qkv, grad, logsum, first, pairs):
    total, width = grad.shape
    return pl.pallas_call(
        functools.partial(backward_kernel, first),
        grid=(pairs,),
        in_specs=[
            pl.BlockSpec(memory_space=pltpu.SMEM),
            whole_block((total, 1)),
            whole_block((1, total)),
            whole_block((total, 3 * width)),
            whole_block((total, width)),
            pl.BlockSpec((1, 2, total), lambda step: (first + step, 0, 0)),
        ],
        out_specs=whole_block((total, 3 * pairs * PAIR)),
        out_shape=jax.ShapeDtypeStruct((total, 3 * pairs * PAIR), BF16),
        scratch_shapes=[
            pltpu.VMEM((total, total), F32),
            pltpu.VMEM((total, PAIR), F32),
            pltpu.VMEM((total, PAIR), F32),
        ],
        compiler_params=pltpu.CompilerParams(vmem_limit_bytes=48 * 1024 * 1024),
        cost_estimate=pl.CostEstimate(
            flops=total * total, bytes_accessed=total * width, transcendentals=0
        ),
        name="attention_backward",
    )(places, seg_keys, seg_queries, qkv, grad, logsum)


def pack_kernel(core, qkv, up, segments, *refs):
    vectors, (send_qkv, keep_qkv, send_up, keep_up) = refs[:-4], refs[-4:]
    rows, width3 = qkv.shape
    half = width3 // 6
    blocks = up.shape[1] // (2 * LANES)
    for place, to_qkv, to_up in ((1 - core[0], send_qkv, send_up), (core[0], keep_qkv, keep_up)):
        for part in range(3):
            start = pl.multiple_of(2 * part * half + place * half, half)
            to_qkv[:, part * half : (part + 1) * half] = qkv[:, pl.ds(start, half)]
        to_qkv[:, 3 * half :] = jnp.zeros((rows, LANES), BF16)
        row = 0
        for vector in vectors:
            count, size = vector.shape
            to_qkv[row : row + count, 3 * half : 3 * half + size] = vector[...]
            row += count
        for sequence in range(segments.shape[0]):
            for start in range(0, segments.shape[1], LANES):
                numbers = segments[sequence : sequence + 1, start : start + LANES]
                to_qkv[row : row + 1, 3 * half :] = numbers.astype(F32).astype(BF16)
                row += 1
        for block in range(blocks):
            start = pl.multiple_of((2 * block + place) * LANES, LANES)
            to_up[:, block * LANES : (block + 1) * LANES] = up[:, pl.ds(start, LANES)]


def pack(core, qkv, up, segments, vectors):
    rows = qkv.shape[0]
    shape_qkv = jax.ShapeDtypeStruct((rows, qkv.shape[1] // 2 + LANES), BF16)
    shape_up = jax.ShapeDtypeStruct((rows, up.shape[1] // 2), BF16)
    vmem = pl.BlockSpec(memory_space=pltpu.VMEM)
    vectors = [vector if vector.ndim == 2 else vector[None] for vector in vectors]
    return pl.pallas_call(
        pack_kernel,
        in_specs=[pl.BlockSpec(memory_space=pltpu.SMEM)] + [vmem] * (3 + len(vectors)),
        out_specs=[vmem] * 4,
        out_shape=[shape_qkv, shape_qkv, shape_up, shape_up],
        name="pack_weights",
    )(core.reshape(1), qkv, up, segments, *vectors)


def beside_kernel(splits, place, line, from_x, from_y, *outs):
    rows = line.shape[1]
    y, x = place[0], place[1]
    for part, py, px in ((line, y, x), (from_x, y, 1 - x), (from_y, 1 - y, x)):
        target = pl.ds(pl.multiple_of((2 * py + px) * rows, rows), rows)
        for out, (start, stop) in zip(outs, splits):
            out[target, :] = part[0, :, start:stop]


def corner_kernel(splits, place, low, high, *refs):
    outs = refs[len(refs) // 2 :]
    half = low.shape[1]
    for out, (start, stop) in zip(outs, splits):
        out[:, 0, :half, :] = low[:, :, start:stop]
        out[:, 0, half:, :] = high[:, :, start:stop]


def put_beside(place, line, from_x, from_y, splits):
    lines, rows, columns = line.shape
    part = pl.BlockSpec((1, rows, columns), lambda step, place: (step, 0, 0))
    return pl.pallas_call(
        functools.partial(beside_kernel, splits),
        grid_spec=pltpu.PrefetchScalarGridSpec(
            num_scalar_prefetch=1,
            grid=(lines,),
            in_specs=[part] * 3,
            out_specs=[
                pl.BlockSpec((4 * rows, stop - start), lambda step, place: (step, 0))
                for start, stop in splits
            ],
        ),
        out_shape=[
            jax.ShapeDtypeStruct((lines * 4 * rows, stop - start), line.dtype)
            for start, stop in splits
        ],
        cost_estimate=pl.CostEstimate(
            flops=6144 * line.size, bytes_accessed=8 * line.size, transcendentals=0
        ),
        name="put_beside",
    )(place, line, from_x, from_y)


def put_corner(place, low, high, wholes, splits):
    lines, half, columns = low.shape

    def there(step, place):
        return (0, 2 * (1 - place[0]) + 1 - place[1], 0, 0)

    part = pl.BlockSpec(low.shape, lambda step, place: (0, 0, 0))
    wholes = [whole.reshape(lines, 4, 2 * half, -1) for whole in wholes]
    return pl.pallas_call(
        functools.partial(corner_kernel, splits),
        grid_spec=pltpu.PrefetchScalarGridSpec(
            num_scalar_prefetch=1,
            grid=(1,),
            in_specs=[part] * 2 + [pl.BlockSpec(memory_space=pl.ANY)] * len(wholes),
            out_specs=[
                pl.BlockSpec((lines, 1, 2 * half, stop - start), there) for start, stop in splits
            ],
        ),
        out_shape=[jax.ShapeDtypeStruct(whole.shape, whole.dtype) for whole in wholes],
        input_output_aliases={3 + place: place for place in range(len(wholes))},
        name="put_corner",
    )(place, low, high, *wholes)


def join_kernel(first, second, out):
    count = first.shape[0]
    out[:count] = first[...]
    out[count:] = second[...]


def join(first, second):
    count, columns = first.shape
    half = pl.BlockSpec((count, columns // 2), lambda step: (0, step))
    return pl.pallas_call(
        join_kernel,
        grid=(2,),
        in_specs=[half, half],
        out_specs=pl.BlockSpec((2 * count, columns // 2), lambda step: (0, step)),
        out_shape=jax.ShapeDtypeStruct((2 * count, columns), first.dtype),
        name="join",
    )(first, second)


def swap_core(array):
    return lax.ppermute(array, "c", SWAP)


def take(array, place, axis=0):
    return lax.dynamic_index_in_dim(array, place, axis, keepdims=False)


def in_order(place, own, other, axis):
    first = jnp.stack([own, other], axis=axis)
    second = jnp.stack([other, own], axis=axis)
    return jnp.where(place == 0, first, second)


def over_x(array):
    count = lax.axis_size("x")
    if count != 2:
        return lax.all_to_all(array, "x", 0, 0)
    here = lax.axis_index("x")
    other = lax.ppermute(take(array, 1 - here), "x", SWAP)
    return in_order(here, take(array, here), other, 0)


def plane_split():
    return tuple(lax.axis_size(name) for name in CHIPS) == (4, 2, 2)


def after(array, *others):
    return lax.optimization_barrier((array, others))[0]


def turn_z(step):
    size = lax.axis_size("z")
    return [(place, (place + step) % size) for place in range(size)]


def gather_line(chunk):
    if not plane_split():
        return chunk
    size, z = lax.axis_size("z"), lax.axis_index("z")
    full = jnp.broadcast_to(chunk, (size,) + chunk.shape)
    for step in range(1, size):
        part = lax.ppermute(chunk, "z", turn_z(step))
        full = lax.dynamic_update_index_in_dim(full, part, (z + size - step) % size, 0)
    return full


def gather_first(line):
    if not plane_split():
        return ()
    return lax.ppermute(line, "x", SWAP), lax.ppermute(line, "y", SWAP)


def gather_second(line, came):
    if not plane_split():
        return ()
    half = line.shape[1] // 2
    from_x, from_y = came
    corner_low = lax.ppermute(from_x[:, :half], "y", SWAP)
    corner_high = lax.ppermute(from_y[:, half:], "x", SWAP)
    return corner_low, corner_high


def gather_whole(line, came, corner, *splits):
    if not plane_split():
        full = lax.all_gather(line, CHIPS).reshape(-1, line.shape[-1])
        return [full[:, start:stop] for start, stop in splits]
    place = jnp.stack([lax.axis_index("y"), lax.axis_index("x")]).astype(jnp.int32)
    wholes = put_beside(place, line, *came, splits)
    wholes = put_corner(place, *corner, wholes, splits)
    return [whole.reshape(-1, whole.shape[-1]) for whole in wholes]


def add_low(*parts):
    return functools.reduce(jnp.add, [part.astype(F32) for part in parts]).astype(BF16)


def plane_turns():
    for step_y, step_x in ((0, 1), (1, 0), (1, 1)):
        turn = [(place, place ^ (2 * step_y + step_x)) for place in range(4)]
        yield step_y, step_x, turn


def plane_part(chunks, step_y, step_x):
    y, x = lax.axis_index("y"), lax.axis_index("x")
    split = chunks.reshape((-1, 4) + chunks.shape[1:])
    return take(split, 2 * (y ^ step_y) + (x ^ step_x), 1)


def scatter_first(chunks):
    if not plane_split():
        return []
    return [
        lax.ppermute(plane_part(chunks, step_y, step_x), ("y", "x"), turn)
        for step_y, step_x, turn in plane_turns()
    ]


def scatter_third(chunks, came):
    return add_terms([plane_part(chunks, 0, 0)] + list(came))


def line_terms(line):
    size, z = lax.axis_size("z"), lax.axis_index("z")
    return [take(line, z)] + [
        lax.ppermute(take(line, (z + step) % size), "z", turn_z(step)) for step in range(1, size)
    ]


def add_terms(terms):
    return functools.reduce(jnp.add, [term.astype(F32) for term in terms])


def scatter_line(line):
    return add_terms(line_terms(line))


def scatter_end(chunks, came, *others):
    if not plane_split():
        return lax.psum_scatter(chunks, CHIPS, scatter_dimension=0).astype(F32)
    return scatter_line(scatter_third(chunks, came).astype(BF16), *others)


def scatter_small(terms):
    return scatter_third(terms, scatter_first(terms))


def per_device(
    inputs,
    segments,
    cotangent,
    ln1_gain,
    ln1_shift,
    qkv_weight,
    qv_bias,
    out_weight,
    out_bias,
    ln2_gain,
    ln2_shift,
    up_weight,
    up_bias,
    down_weight,
    down_bias,
):
    _, rows, width = inputs.shape
    own_rows = out_weight.shape[0]
    own_units = down_weight.shape[0]
    chips = width // (2 * own_rows)
    core = lax.axis_index("c")
    half = width // 2
    mine = 2 * chips * own_units // 2

    seg_rows = segments.size // LANES
    in_rows = own_units % LANES == 0 and rows % LANES == 0 and own_rows >= 9 + seg_rows
    if in_rows:
        vectors = (ln1_gain, ln1_shift, qv_bias, out_bias, ln2_gain, ln2_shift, down_bias, up_bias)
        packed = pack(core, qkv_weight, up_weight, segments, vectors)
    else:
        small = jnp.concatenate(
            [ln1_gain, ln1_shift, qv_bias[0], qv_bias[1], out_bias, ln2_gain, ln2_shift, down_bias]
            + [up_bias]
        )
        small_count = small.shape[0]
        small = jnp.pad(small, (0, own_rows * LANES - small_count)).reshape(own_rows, LANES)

        def head_columns(place):
            columns = [
                lax.dynamic_slice_in_dim(qkv_weight, part * width + place * half, half, 1)
                for part in range(3)
            ]
            return jnp.concatenate(columns + [small], axis=1)

        up_split = up_weight.reshape(own_rows, chips, 2, own_units)
        packed = (
            head_columns(1 - core),
            head_columns(core),
            take(up_split, 1 - core, 2).reshape(own_rows, mine),
            take(up_split, core, 2).reshape(own_rows, mine),
        )
    send_qkv, keep_qkv, send_up, keep_up = packed
    chunk_qkv = in_order(core, keep_qkv, swap_core(send_qkv), 0).reshape(2 * own_rows, -1)
    send_up = after(send_up, chunk_qkv)
    chunk_up = in_order(core, keep_up, swap_core(send_up), 0).reshape(2 * own_rows, -1)
    chunk_out = jnp.concatenate([out_weight[:, :half], out_weight[:, half:]], axis=0)
    chunk_up = jnp.concatenate([chunk_up, chunk_out], axis=1)

    def both_cores(own):
        return join(own, swap_core(own))

    def joined(array):
        return array.reshape((-1,) + array.shape[2:])

    line_qkv = gather_line(chunk_qkv)
    if lax.axis_size("x") == 2:
        here = lax.axis_index("x")
        other = lax.ppermute(take(inputs, 1 - here), "x", SWAP)
        own_x = in_order(here, take(inputs, here), other, 0)
    else:
        own_x = over_x(inputs)
    own_x = joined(own_x)
    total = 2 * own_x.shape[0]
    pieces = jnp.arange(total // rows, dtype=jnp.int32)
    places = jnp.where(pieces % 2 == core, 0, own_x.shape[0]) + pieces // 2 * rows

    line_up = lax.all_gather(chunk_up, "z") if plane_split() else chunk_up
    line_qkv = after(line_qkv, own_x, chunk_up)
    came_qkv = gather_first(line_qkv)
    full_x = both_cores(own_x)
    line_down, came_down = down_weight[None], ()
    if plane_split():
        line_down = after(line_down, came_qkv)
        came_down = gather_first(line_down)
    full_x = full_x.astype(F32)
    corner_qkv = gather_second(line_qkv, came_qkv)
    plane_down = down_weight
    if plane_split():
        corner_down = gather_second(line_down, came_down)
        plane_down = gather_whole(line_down, came_down, corner_down, (0, width))[0]
    corner_qkv, plane_down = lax.optimization_barrier((corner_qkv, plane_down))
    w_qkv, smalls = gather_whole(
        line_qkv, came_qkv, corner_qkv, (0, 3 * half), (3 * half, 3 * half + LANES)
    )
    smalls = smalls.reshape(2 * chips, own_rows, LANES)
    if in_rows:
        vectors = [smalls[:, place, :own_rows] for place in range(8)]
        small_up = smalls[:, 8, :own_units]
    else:
        smalls = smalls.reshape(2 * chips, -1)
        vectors = [smalls[:, place * own_rows : (place + 1) * own_rows] for place in range(8)]
        small_up = smalls[:, 8 * own_rows : 8 * own_rows + own_units]
    vectors = [vector.reshape(width).astype(F32) for vector in vectors]
    if in_rows:
        seg_all = smalls[:, 9 : 9 + seg_rows].reshape(-1, lax.axis_size("x"), 2, segments.size)
        seg_all = take(seg_all, lax.axis_index("z") * lax.axis_size("y") + lax.axis_index("y"))
        seg_all = seg_all.reshape((-1, 2) + segments.shape)
        seg_all = take(seg_all, lax.axis_index("x"), 2).reshape(-1).astype(jnp.int32)
    else:
        own_seg = over_x(segments)
        seg_all = in_order(core, own_seg, swap_core(own_seg), 1).reshape(-1)
    seg_keys = seg_all[:, None]
    seg_queries = seg_all[None, :]
    gain1, shift1, b_q, b_v, b_out, gain2, shift2, b_down = vectors
    b_up = take(small_up.reshape(chips, 2, own_units), core, 1)
    b_up = b_up.reshape(mine).astype(F32)

    normed1 = norm_forward(full_x, gain1, shift1).astype(BF16)
    normed1, line_up = lax.optimization_barrier((normed1, line_up))
    b_qkv = jnp.concatenate(
        [
            lax.dynamic_slice_in_dim(b_q, core * half, half),
            jnp.zeros((half,), F32),
            lax.dynamic_slice_in_dim(b_v, core * half, half),
        ]
    )
    qkv = (dot_plain(normed1, w_qkv) + b_qkv).astype(BF16)
    w_down = lax.all_gather(plane_down, "z" if plane_split() else CHIPS).reshape(mine, width)
    line_up = after(line_up, corner_qkv)
    came_up = gather_first(line_up)
    attended, logsum = attend(places, seg_keys, seg_queries, qkv)
    attended = after(attended, came_up)
    came_up = after(came_up, attended)
    corner_up = gather_second(line_up, came_up)
    w_up, all_out = gather_whole(
        line_up, came_up, corner_up, (0, mine), (mine, mine + half)
    )
    all_out = all_out.reshape(chips, 2 * own_rows, half)
    all_out = jnp.concatenate([all_out[:, :own_rows], all_out[:, own_rows:]], axis=2)
    out_keep = lax.dynamic_slice_in_dim(all_out, core * (chips // 2), chips // 2)
    out_send = lax.dynamic_slice_in_dim(all_out, (1 - core) * (chips // 2), chips // 2)
    w_out = in_order(core, out_keep, swap_core(out_send), 1).reshape(half, width)

    def add_cores(dot, left, weight):
        count = left.shape[0] // 2
        other = swap_core(dot(left[count:], weight).astype(BF16))
        return dot(left[:count], weight) + other.astype(F32)

    own_g = joined(over_x(after(cotangent, came_up)))
    attended, own_g = lax.optimization_barrier((attended, own_g))
    resid = own_x.astype(F32) + add_cores(dot_plain, attended, w_out) + b_out
    normed2_own = norm_forward(resid, gain2, shift2).astype(BF16)
    normed2 = both_cores(normed2_own)
    normed2, w_down = lax.optimization_barrier((normed2, w_down))
    full_g = both_cores(own_g)
    pre = dot_plain(normed2, w_up) + b_up
    active, gelu_pull = jax.vjp(gelu_tanh, pre)
    active = active.astype(BF16)
    slope = gelu_pull(jnp.ones_like(pre))[0].astype(BF16)
    active, slope = lax.optimization_barrier((active, slope))
    grad_down = dot_outer(active, full_g).astype(BF16).reshape(chips, own_units, width)
    full_g, grad_down = lax.optimization_barrier((full_g, grad_down))
    if plane_split():
        line_gd = lax.psum_scatter(
            grad_down.reshape(-1, 4, own_units, width), "z", scatter_dimension=0
        )
    else:
        line_gd = grad_down
    grad_active = dot_back(full_g, w_down)
    grad_pre = (grad_active * slope.astype(F32)).astype(BF16)
    up_terms = dot_outer(normed2, grad_pre).astype(BF16).reshape(chips, 2 * own_rows, mine)
    grad_pre, up_terms = lax.optimization_barrier((grad_pre, up_terms))
    came_gu = scatter_first(up_terms)
    grad_normed2 = add_cores(dot_back, grad_pre, w_up)
    own_g32 = own_g.astype(F32)
    _, norm2_pull = jax.vjp(norm_forward, resid, gain2, shift2)
    grad_part, grad_gain2, grad_shift2 = norm2_pull(grad_normed2)
    grad_resid = own_g32 + grad_part

    grad_branch_own = grad_resid.astype(BF16)
    grad_branch = both_cores(grad_branch_own)
    grad_attended = dot_back(grad_branch, w_out).astype(BF16)
    grad_out = dot_outer(attended, grad_branch).astype(BF16)
    grad_out = grad_out.reshape(chips // 2, 2, own_rows, width)
    out_other = swap_core(take(grad_out, 1 - core, 1))
    out_terms = in_order(core, take(grad_out, core, 1), out_other, 0)
    out_terms = out_terms.reshape(chips, own_rows, width)
    out_terms = jnp.concatenate([out_terms[..., :half], out_terms[..., half:]], axis=1)
    pairs = half // PAIR
    few = pairs // 2
    grad_low = attend_back(places, seg_keys, seg_queries, qkv, grad_attended, logsum, 0, few)
    low_terms = dot_outer(normed1, grad_low).astype(BF16).reshape(chips, 2 * own_rows, -1)
    low_terms = jnp.concatenate([low_terms, out_terms], axis=2)
    grad_attended, low_terms = lax.optimization_barrier((grad_attended, low_terms))
    came_low = scatter_first(low_terms)
    grad_high = attend_back(
        places, seg_keys, seg_queries, qkv, grad_attended, logsum, few, pairs - few
    )
    came_gu, grad_high, grad_low, line_gd = lax.optimization_barrier(
        (came_gu, grad_high, grad_low, line_gd)
    )
    if plane_split():
        line_gu = scatter_third(up_terms, came_gu).astype(BF16)
    else:
        line_gu = up_terms
    high_terms = dot_outer(normed1, grad_high).astype(BF16).reshape(chips, 2 * own_rows, -1)
    high_terms = [high_terms]
    if plane_split():
        down_terms = line_gd.reshape(4, -1, own_rows, width)
        down_terms = jnp.concatenate([down_terms[..., :half], down_terms[..., half:]], axis=2)
        down_terms = down_terms.transpose(1, 0, 2, 3).reshape(chips, 2 * own_rows, half)
        high_terms.append(down_terms)
    high_terms = jnp.concatenate(high_terms, axis=2)
    came_high = scatter_first(high_terms)
    near_low, high_terms, active = lax.optimization_barrier((came_low[:2], high_terms, active))
    came_low = list(near_low) + came_low[2:]
    mixed = add_cores(dot_plain, active, w_down) + b_down
    outputs = (resid + mixed).astype(BF16).reshape(-1, rows, width)

    low_width, high_width = few * PAIR, (pairs - few) * PAIR
    w_low = jnp.concatenate(
        [w_qkv[:, part * half : part * half + low_width] for part in range(3)], axis=1
    )
    w_high = jnp.concatenate(
        [w_qkv[:, part * half + low_width : (part + 1) * half] for part in range(3)], axis=1
    )
    count = grad_low.shape[0] // 2
    other = dot_back(grad_low[count:], w_low) + dot_back(grad_high[count:], w_high)
    other = swap_core(other.astype(BF16)).astype(F32)
    grad_normed1 = dot_back(grad_low[:count], w_low) + dot_back(grad_high[:count], w_high) + other
    own_x32 = own_x.astype(F32)
    _, norm1_pull = jax.vjp(norm_forward, own_x32, gain1, shift1)
    grad_part1, grad_gain1, grad_shift1 = norm1_pull(grad_normed1)
    grad_x = (grad_resid + grad_part1).reshape(-1, rows, width)

    def place_heads(sums):
        zeros = jnp.zeros((width,), F32)
        return lax.dynamic_update_slice_in_dim(zeros, sums, core * half, 0)

    low_sums = jnp.sum(grad_low.astype(F32), axis=0)
    high_sums = jnp.sum(grad_high.astype(F32), axis=0)

    def head_sums(part):
        low = low_sums[part * low_width : (part + 1) * low_width]
        high = high_sums[part * high_width : (part + 1) * high_width]
        return place_heads(jnp.concatenate([low, high]))

    small_sums = [
        grad_gain1,
        grad_shift1,
        head_sums(0),
        head_sums(2),
        jnp.sum(grad_branch_own.astype(F32), axis=0),
        grad_gain2,
        grad_shift2,
        jnp.sum(own_g32, axis=0),
    ]
    up_sums = jnp.sum(grad_pre.astype(F32), axis=0)
    small_terms = jnp.concatenate(
        [vector.reshape(chips, 2 * own_rows) for vector in small_sums]
        + [up_sums.reshape(chips, own_units)],
        axis=1,
    )
    small_width = small_terms.shape[1]
    small_terms = jnp.pad(small_terms, ((0, 0), (0, 2 * own_rows * LANES - small_width)))
    small_terms = small_terms.reshape(chips, 2 * own_rows, LANES)

    low_got = []
    if plane_split():
        line_low = scatter_third(low_terms, came_low).astype(BF16)
        low_got = line_terms(line_low)
        up_sum = lax.psum_scatter(line_gu, "z", scatter_dimension=0).astype(F32)
    came_high, low_got, small_terms = lax.optimization_barrier((came_high, low_got, small_terms))

    count = lax.axis_size("x")
    if count == 2:
        here = lax.axis_index("x")
        other = lax.ppermute(take(grad_x, 1 - here).astype(BF16), "x", SWAP)
        other, outputs = lax.optimization_barrier((other, outputs))
        input_grad = in_order(here, take(grad_x, here), other.astype(F32), 0)
    else:
        input_grad = over_x(grad_x)
    if plane_split():
        low_sum = add_terms(low_got)
        line_high = scatter_third(high_terms, came_high)
        down_grad = line_high[..., 3 * high_width :]
        down_grad = jnp.concatenate([down_grad[:, :own_rows], down_grad[:, own_rows:]], axis=2)
        down_grad = down_grad.reshape(own_units, width)
        line_high = line_high[..., : 3 * high_width]
        line_high = jnp.concatenate([line_high, scatter_small(small_terms)], axis=2).astype(BF16)
        outputs = over_x(after(outputs, came_high))
        high_got = line_terms(line_high)
        high_got, input_grad, outputs = lax.optimization_barrier((high_got, input_grad, outputs))
        high_sum = add_terms(high_got)
    else:
        down_grad = lax.psum_scatter(line_gd, CHIPS, scatter_dimension=0).astype(F32)
        low_sum = scatter_end(low_terms, ())
        up_sum = scatter_end(up_terms, ())
        outputs = over_x(outputs)
        high_sum = scatter_end(jnp.concatenate([high_terms.astype(F32), small_terms], axis=2), ())
    out_sum = low_sum[:, 3 * low_width :]
    qkv_sum = jnp.concatenate(
        [
            piece
            for part in range(3)
            for piece in (
                low_sum[:, part * low_width : (part + 1) * low_width],
                high_sum[:, part * high_width : (part + 1) * high_width],
            )
        ],
        axis=1,
    )
    sums = high_sum[:, 3 * high_width :].reshape(-1)
    up_sum = up_sum.reshape(2, own_rows, mine)
    out_grad = jnp.concatenate([out_sum[:own_rows], out_sum[own_rows:]], axis=1)
    up_other = swap_core(take(up_sum, 1 - core))
    up_grad = in_order(
        core,
        take(up_sum, core).reshape(own_rows, chips, own_units),
        up_other.reshape(own_rows, chips, own_units),
        2,
    )
    up_grad = up_grad.reshape(own_rows, 2 * mine)
    weight_sum = qkv_sum.reshape(2, own_rows, 3 * half)
    qkv_other = swap_core(take(weight_sum, 1 - core))
    qkv_grad = in_order(
        core,
        take(weight_sum, core).reshape(own_rows, 3, half),
        qkv_other.reshape(own_rows, 3, half),
        2,
    )
    qkv_grad = qkv_grad.reshape(own_rows, 6 * half)
    shared = sums[: 16 * own_rows].reshape(8, 2, own_rows)
    shared = take(shared, core, 1) + swap_core(take(shared, 1 - core, 1))
    up_bias_grad = sums[16 * own_rows : 16 * own_rows + own_units]

    return (
        outputs,
        input_grad,
        shared[0],
        shared[1],
        qkv_grad,
        shared[2:4],
        out_grad,
        shared[4],
        shared[5],
        shared[6],
        up_grad,
        up_bias_grad,
        down_grad,
        shared[7],
    )


def solution(mesh):
    groups, members = mesh.devices.shape
    split = Mesh(mesh.devices.reshape(groups // 2, 2, members // 2, 2), ("z", "y", "x", "c"))
    every = ("z", "y", "x", "c")
    tokens = P(("z", "y"), ("x", "c"), None)
    vector = P(every)
    matrix = P(every, None)
    return jax.shard_map(
        per_device,
        mesh=split,
        in_specs=(
            tokens,
            P(("z", "y"), ("x", "c")),
            tokens,
            vector,
            vector,
            matrix,
            P(None, every),
            matrix,
            vector,
            vector,
            vector,
            matrix,
            vector,
            matrix,
            vector,
        ),
        out_specs=(
            tokens,
            tokens,
            vector,
            vector,
            matrix,
            P(None, every),
            matrix,
            vector,
            vector,
            vector,
            matrix,
            vector,
            matrix,
            vector,
        ),
        check_vma=False,
    )
```
